256 devices in a mesh: dp: 16 (over y, x), dim: 16 (over z, core).
Axes of the slice: x: 4, y: 4, z: 8, core: 2. Of those that a mesh axis runs over, the one named last changes fastest.
Arguments:
- vectors: float32 [128, 65536], P('dim', 'dp'), may hold values from -192 to 192
- code_ids: int32 [8, 65536], P(None, 'dp'), may hold values from 0 to 255
- start_books: float32 [8, 128, 256], P(None, 'dim'), may hold values from -6 to 6
Outputs:
- codebooks: float32 [8, 128, 256], P(None, 'dim')
- residual: float32 [8, 128, 256], P(None, 'dim')
The draws below stay inside these ranges and needn't reach their ends.
All inputs are finite; a program needn't handle non-finite values.
Results may differ from the reference program's by a relative error of at most 0.002.
Values sent between devices are 32-bit elements; how exact they have to be, the bound alone decides.
A program may use at most 64 MiB of HBM per device.

```python
import math
import jax
import jax.numpy as jnp
import numpy as np

M = 8
K = 256
DIMS = 128
ITERS = 3
NTOT = 65536


def with_ends(values, stream_key, low, top_value):
    shape = values.shape
    index_at = [jax.random.randint(jax.random.fold_in(stream_key, axis), (), 0, shape[axis]) for axis in range(len(shape))]
    values = values.at[tuple(index_at)].set(low)
    longest = shape.index(max(shape))
    index_at[longest] = (index_at[longest] + 1) % shape[longest]
    return values.at[tuple(index_at)].set(top_value)


def levels(key, dims, pieces, smallest, top_value):
    gain = 1.0
    for position, parts in pieces:
        heights = jax.random.uniform(jax.random.fold_in(jax.random.fold_in(key, 6), position), (parts,), jnp.float32, smallest / len(pieces), top_value / len(pieces))
        gain = gain * jnp.repeat(jnp.exp(heights), dims[position] // parts).reshape((-1,) + (1,) * (len(dims) - 1 - position))
    return gain


def rank_bounds(count, skew):
    weights = [(1 << 20) // math.isqrt(rank ** skew) + 1 for rank in range(1, count + 1)]
    scale = 1 + sum(weights) // (1 << 30)
    return np.cumsum(np.array([max(1, weight // scale) for weight in weights]))


def ranked_ids(stream_key, extent, amount, skew):
    table = rank_bounds(amount, skew)
    ticket = jax.random.randint(jax.random.fold_in(stream_key, 1), extent, 0, int(table[amount - 1]))
    rank = jnp.searchsorted(jnp.asarray(table, jnp.int32), ticket, side="right")
    return jax.random.permutation(jax.random.fold_in(stream_key, 2), amount)[rank].astype(jnp.int32)


def centred(key, extent, width, bound, pieces=(), held_as=jnp.bfloat16):
    loudness = levels(key, extent, pieces, -0.22, 0.18) if pieces else 1.0
    drawn = jax.random.normal(key, extent, jnp.float32) * width * loudness
    return jnp.minimum(jnp.maximum(drawn, -bound), bound).astype(held_as)


def setup_inputs(seed: int = 0) -> dict:
    keys = jax.random.split(jax.random.key(seed), 4)
    return {
        "vectors": centred(keys[0], (DIMS, NTOT), 32.0, 192.0, ((0, 16), (1, 16)), jnp.float32),
        "code_ids": with_ends(ranked_ids(keys[1], (M, NTOT), K, 1), jax.random.fold_in(keys[1], 3), 0, K - 1).astype(jnp.int32),
        "start_books": centred(keys[2], (M, DIMS, K), 1.0, 6.0, ((1, 16),), jnp.float32),
    }


ridge = 0.5


def rebuild(codebook, code_ids):
    rebuilt = jnp.zeros((codebook.shape[1], code_ids.shape[1]), codebook.dtype)
    for section in range(M):
        rebuilt = rebuilt + jnp.take(codebook[section], code_ids[section], axis=1)
    return rebuilt


def collect(differ, code_ids):
    return jnp.stack([jax.ops.segment_sum(differ.T, code_ids[section], num_segments=K).T for section in range(M)])


def operate(codebook, code_ids):
    return (K / NTOT) * collect(rebuild(codebook, code_ids), code_ids) + ridge * codebook


def reference(vectors, code_ids, start_books):
    codebook = start_books
    residual = (K / NTOT) * collect(vectors - rebuild(start_books, code_ids), code_ids) - ridge * start_books
    direction = residual
    norm_now = jnp.sum(residual * residual)
    for turn in range(ITERS):
        image = operate(direction, code_ids)
        step_len = norm_now / jnp.sum(direction * image)
        codebook = codebook + step_len * direction
        residual = residual - step_len * image
        norm_next = jnp.sum(residual * residual)
        direction = residual + (norm_next / norm_now) * direction
        norm_now = norm_next
    return codebook, residual
```

```python
import functools

import jax
import jax.numpy as jnp
from jax import lax
from jax.experimental import pallas as pl
from jax.experimental.pallas import tpu as pltpu
from jax.sharding import PartitionSpec as P

f32 = jnp.float32
bf16 = jnp.bfloat16
MESH = pl.DeviceIdType.MESH
LANES = 128
SECTIONS = 8
CODES = 256
RIDGE = 0.5
SHIFT = 2.0


def two_sum(a, b):
    s = a + b
    t = s - a
    return s, (a - (s - t)) + (b - t)


def two_prod(a, b):
    p = a * b
    ca = a * 4097.0
    ah = ca - (ca - a)
    al = a - ah
    cb = b * 4097.0
    bh = cb - (cb - b)
    bl = b - bh
    return p, ((ah * bh - p) + ah * bl + al * bh) + al * bl


def tidy(h, r):
    s = h + r
    return s, r - (s - h)


def plus(a, b):
    s, e = two_sum(a[0], b[0])
    return tidy(s, e + (a[1] + b[1]))


def minus(a, b):
    return plus(a, (-b[0], -b[1]))


def times(a, b):
    p, e = two_prod(a[0], b[0])
    return tidy(p, e + (a[0] * b[1] + a[1] * b[0]))


def over(a, b):
    first = a[0] / b[0]
    rest = minus(a, times((first, jnp.zeros_like(first)), b))
    return tidy(first, rest[0] / b[0])


def scaled(a, power):
    return a[0] * power, a[1] * power


def pick(table, index):
    place = index & (LANES - 1)
    low = jnp.take_along_axis(table[0], place, axis=1)
    high = jnp.take_along_axis(table[1], place, axis=1)
    return jnp.where(index >= LANES, high, low)


def make_masks(ids_ref, low_ref, high_ref, chunk=1024):
    count = ids_ref.shape[1]
    row_low = lax.broadcasted_iota(jnp.int32, (64, chunk), 0) & 7
    row_high = lax.broadcasted_iota(jnp.int32, (CODES, chunk), 0) & 31

    def step(k, carry):
        span = pl.ds(pl.multiple_of(k * chunk, chunk), chunk)
        code = ids_ref[:, span]
        top = code >> 5
        wide = jnp.concatenate(
            [jnp.broadcast_to(top[m : m + 1], (8, chunk)) for m in range(SECTIONS)], axis=0
        )
        low_ref[:, span] = jnp.where(wide == row_low, 1.0, 0.0).astype(bf16)
        part = code & 31
        wide = jnp.concatenate(
            [jnp.broadcast_to(part[m : m + 1], (32, chunk)) for m in range(SECTIONS)], axis=0
        )
        high_ref[span, :] = jnp.where(wide == row_high, 1.0, 0.0).astype(bf16).T
        return carry

    lax.fori_loop(0, count // chunk, step, 0)


def forward_local(books_ref, vec_ref, ids_ref, e_ref):
    count = ids_ref.shape[1]

    def step(g, carry):
        span = pl.ds(pl.multiple_of(g * LANES, LANES), LANES)
        code = ids_ref[:, span]
        total = vec_ref[:, span]
        for m in range(SECTIONS):
            total = total - pick(
                (books_ref[0, 8 * m : 8 * m + 8, :], books_ref[1, 8 * m : 8 * m + 8, :]), jnp.broadcast_to(code[m : m + 1], (8, LANES))
            )
        e_ref[:, span] = total
        return carry

    lax.fori_loop(0, count // LANES, step, 0, unroll=4)


def forward(table, ids_ref, e_ref, packed=False):
    count = ids_ref.shape[1]
    row = lax.broadcasted_iota(jnp.int32, (8, LANES), 0)
    blocks = []
    table = (table[:, :LANES], table[:, LANES:])
    for g in range(count // LANES):
        span = slice(g * LANES, (g + 1) * LANES)
        e = jnp.sum(pick(table, ids_ref[:, span]), axis=0, keepdims=True)
        e_ref[:, span] = e
        if packed:
            wide = jnp.broadcast_to(e, (8, LANES))
            if g % 8 == 0:
                blocks.append(wide)
            else:
                blocks[-1] = jnp.where(row == g % 8, wide, blocks[-1])
    return blocks


def weighted(low, e_row):
    wide = jnp.broadcast_to(e_row, (16, e_row.shape[1]))
    first = wide.astype(bf16)
    second = (wide - first.astype(f32)).astype(bf16)
    return jnp.concatenate(
        [low * jnp.concatenate([first] * 4, axis=0), low * jnp.concatenate([second] * 4, axis=0)],
        axis=0,
    )


def backward(low_ref, high_ref, e_ref, size=2048):
    total = None
    for q in range(low_ref.shape[1] // size):
        span = slice(q * size, (q + 1) * size)
        rows = weighted(low_ref[:, span], e_ref[:, span])
        term = jnp.dot(rows, high_ref[span, :], preferred_element_type=f32)
        total = term if total is None else total + term
    return total


def extract(acc, fold_ref):
    both = acc[:64] + acc[64:]
    for m in range(SECTIONS):
        half = both[8 * m : 8 * m + 8, :LANES] if m < 4 else both[8 * m : 8 * m + 8, LANES:]
        fold_ref[8 * m : 8 * m + 8, :] = half if m % 4 == 0 else pltpu.roll(half, LANES - 32 * (m % 4), 1)
    block = lax.broadcasted_iota(jnp.int32, (8, LANES), 1) >> 5
    halves = []
    for h in range(2):
        out = None
        for q in range(4):
            piece = fold_ref[pl.ds(4 * h + q, 8, stride=8), :]
            out = piece if q == 0 else jnp.where(block == q, pltpu.roll(piece, 32 * q, 1), out)
        halves.append(out)
    return jnp.concatenate(halves, axis=1)


def dot_rows(pairs, extra):
    row = lax.broadcasted_iota(jnp.int32, (8, LANES), 0)
    found = []
    for a, b in pairs:
        left = two_prod(a[:, :LANES], b[:, :LANES])
        right = two_prod(a[:, LANES:], b[:, LANES:])
        found.append(scaled(plus(left, right), 0.5))
    found.append(extra)
    high = jnp.zeros((8, LANES), f32)
    rest = jnp.zeros((8, LANES), f32)
    for q, pair in enumerate(found):
        for distance in (4, 2, 1):
            pair = plus(pair, (pltpu.roll(pair[0], distance, 0), pltpu.roll(pair[1], distance, 0)))
        high = jnp.where(row == q, pair[0], high)
        rest = jnp.where(row == q, pair[1], rest)
    pair = (high, rest)
    for distance in (64, 32, 16, 8, 4, 2, 1):
        pair = plus(pair, (pltpu.roll(pair[0], distance, 1), pltpu.roll(pair[1], distance, 1)))
    return pair


def tree(terms):
    while len(terms) > 1:
        terms = [plus(terms[k], terms[k + 1]) for k in range(0, len(terms), 2)]
    return terms[0]


def solve(total, scale):
    d00, d01, d02, d11, d12, d22, norm = [(total[0][q : q + 1], total[1][q : q + 1]) for q in range(7)]
    w00 = plus(d01, scaled(d00, SHIFT))
    w01 = plus(d02, scaled(d01, SHIFT))
    w02 = plus(d12, scaled(d02, SHIFT))
    w11 = plus(d12, scaled(d11, SHIFT))
    w12 = plus(d22, scaled(d12, SHIFT))
    w22 = plus(scaled(norm, scale), scaled(d22, RIDGE))
    l1 = over(w01, w00)
    l2 = over(w02, w00)
    p1 = minus(w11, times(l1, w01))
    u12 = minus(w12, times(l2, w01))
    l3 = over(u12, p1)
    p2 = minus(minus(w22, times(l2, w02)), times(l3, u12))
    y1 = minus(d01, times(l1, d00))
    y2 = minus(minus(d02, times(l2, d00)), times(l3, y1))
    c2 = over(y2, p2)
    c1 = minus(over(y1, p1), times(l3, c2))
    c0 = minus(minus(over(d00, w00), times(l1, c1)), times(l2, c2))
    return c0, c1, c2


def kernel(
    planes, scale, vec_hbm, ids_hbm, books_hbm, x_ref, r_ref,
    vec, books, ids, low, high, e_local, e_rows, fold, acc,
    rs_out, rs_in, pair_out, pair_in, base, base_in, last_in,
    z_out, z_in, s_out, s_in,
    in_sem, ids_send, ids_recv, rs_send, rs_recv, pair_send, pair_recv,
    ag_send, ag_recv, z_send, z_recv, s_send, s_recv,
):
    dp = lax.axis_index("dp")
    dim = lax.axis_index("dim")
    core = dim % 2
    plane = dim // 2
    owner = dp // 8
    slot = dp % 8
    owned = core == owner
    half = ids.shape[2] // 2
    devices = 2 * planes

    def remote(src, dst, send_sem, recv_sem, target):
        return pltpu.make_async_remote_copy(
            src_ref=src, dst_ref=dst, send_sem=send_sem, recv_sem=recv_sem,
            device_id=target, device_id_type=MESH,
        )

    inputs = [
        pltpu.make_async_copy(ids_hbm, ids.at[8], in_sem.at[0]),
        pltpu.make_async_copy(books_hbm, books, in_sem.at[1]),
        pltpu.make_async_copy(vec_hbm, vec, in_sem.at[2]),
    ]
    for copy in inputs:
        copy.start()

    barrier = pltpu.get_barrier_semaphore()

    def greet_plane(k, carry):
        target = ((dp + k // 2) % 16, 2 * plane + (core + k) % 2)
        pl.semaphore_signal(barrier, inc=1, device_id=target, device_id_type=MESH)
        return carry

    def greet_line(k, carry):
        target = (dp, 2 * ((plane + k // 2) % planes) + k % 2)
        pl.semaphore_signal(barrier, inc=1, device_id=target, device_id_type=MESH)
        return carry

    lax.fori_loop(1, 32, greet_plane, 0)
    lax.fori_loop(2, devices, greet_line, 0)

    def ids_part(where, which):
        return ids.at[where, :, pl.ds(pl.multiple_of(which * half, half), half)]

    def ids_copy(k):
        return remote(
            ids_part(8, core), ids_part(slot, core), ids_send.at[k], ids_recv.at[slot, core],
            ((dp + k) % 16, 2 * plane + owner),
        )

    def ids_arrival(where, which):
        return remote(
            ids_part(8, which), ids_part(where, which), ids_send.at[0], ids_recv.at[where, which],
            (dp, 2 * plane + 1 - core),
        )

    def rs_copy(d, other):
        return remote(
            rs_out.at[d], rs_in.at[dp], rs_send.at[d, other], rs_recv.at[dp],
            (8 * core + d, 2 * plane + other),
        )

    def rs_away(d, other):
        return jnp.logical_or(8 * core + d != dp, other != core)

    def pair_copy(p):
        return remote(
            pair_out.at[p], pair_in.at[p], pair_send.at[p], pair_recv.at[p], (dp, 2 * plane + 1 - core)
        )

    def ag_copy(which, k):
        target = ((dp + k) % 16, dim)
        if which == 0:
            return remote(base.at[pl.ds(0, 3)], base_in.at[slot], ag_send.at[0, k], ag_recv.at[0, slot], target)
        return remote(base.at[3], last_in.at[slot], ag_send.at[1, k], ag_recv.at[1, slot], target)

    def ag_arrival(which, r):
        target = ((dp + 1) % 16, dim)
        if which == 0:
            return remote(base.at[pl.ds(0, 3)], base_in.at[r], ag_send.at[0, 0], ag_recv.at[0, r], target)
        return remote(base.at[3], last_in.at[r], ag_send.at[1, 0], ag_recv.at[1, r], target)

    def z_copy(k):
        return remote(z_out, z_in.at[dim], z_send.at[k], z_recv.at[dim], (dp, (dim + k) % devices))

    def z_arrival(k):
        return remote(z_out, z_in.at[k], z_send.at[0], z_recv.at[k], (dp, (dim + 1) % devices))

    def s_copy(k):
        return remote(s_out, s_in.at[dp], s_send.at[k], s_recv.at[dp], ((dp + k) % 16, dim))

    def s_arrival(k):
        return remote(s_out, s_in.at[k], s_send.at[0], s_recv.at[k], ((dp + 1) % 16, dim))

    def each(low_end, high_end, act):
        lax.fori_loop(low_end, high_end, lambda k, carry: (act(k), carry)[1], 0)

    def unless(skip, act):
        pl.when(jnp.logical_not(skip))(act)

    inputs[0].wait()
    make_masks(ids.at[8], low.at[8], high.at[8])
    inputs[1].wait()
    inputs[2].wait()
    forward_local(books, vec, ids.at[8], e_local)
    for d in range(8):
        e_rows[d] = e_local[d : d + 1, :]
        for h in range(2):
            rs_out[d, :, h * LANES : (h + 1) * LANES] = (RIDGE / 16) * books[h, pl.ds(d, 8, stride=8), :]

    pl.semaphore_wait(barrier, 31 + devices - 2)
    each(1, 16, lambda k: ids_copy(k).start())

    def local_pass(d, carry):
        found = extract(backward(low.at[8], high.at[8], e_rows.at[d]), fold)
        rs_out[d] = scale * found - rs_out[d]
        for other in range(2):
            pl.when(rs_away(d, other))(lambda: rs_copy(d, other).start())
        return carry

    lax.fori_loop(0, 8, local_pass, 0)

    @pl.when(owned)
    def _():
        rs_in[dp] = rs_out[slot]

    each(0, 16, lambda k: unless(jnp.logical_and(owned, k == dp), lambda: remote(
        rs_out.at[0], rs_in.at[k], rs_send.at[0, 0], rs_recv.at[k], (dp, 2 * plane + 1 - core)).wait_recv()))
    terms = [rs_in[k] for k in range(16)]
    while len(terms) > 1:
        terms = [terms[k] + terms[k + 1] for k in range(0, len(terms), 2)]
    base[0] = terms[0]

    def join(p, found):
        pair_out[p] = scale * found
        pair_copy(p).start()

    def joined(p):
        pair_copy(p).wait_recv()
        base[p + 1] = (pair_out[p] + pair_in[p]) + (RIDGE - SHIFT) * base[p]

    def place(q):
        return jnp.where(jnp.logical_and(owned, q == 0), 8, (slot + q) % 8)

    acc[...] = jnp.zeros_like(acc)

    def first_pass(q, carry):
        where = place(q)

        @pl.when(where < 8)
        def _():
            ids_arrival(where, 0).wait_recv()
            ids_arrival(where, 1).wait_recv()
            make_masks(ids.at[where], low.at[where], high.at[where])

        forward(base[0], ids.at[where], e_rows.at[q])
        acc[...] += backward(low.at[where], high.at[where], e_rows.at[q])
        return carry

    lax.fori_loop(0, 8, first_pass, 0)
    join(0, extract(acc[...], fold))
    joined(0)

    def sweep():
        def two(q, total):
            first, second = place(2 * q), place(2 * q + 1)
            one = backward(low.at[first], high.at[first], e_rows.at[2 * q])
            other = backward(low.at[second], high.at[second], e_rows.at[2 * q + 1])
            return total + (one + other)

        return lax.fori_loop(0, 4, two, jnp.zeros((128, CODES), f32))

    each(0, 8, lambda q: forward(base[1], ids.at[place(q)], e_rows.at[q]))
    join(1, extract(sweep(), fold))
    joined(1)

    @pl.when(owned)
    def _():
        each(1, 16, lambda k: ag_copy(0, k).start())
        base_in[slot] = base[0:3]

    def last_forward(q, carry):
        blocks = forward(base[2], ids.at[place(q)], e_rows.at[q], packed=True)
        for block in blocks:
            carry = plus(carry, two_prod(block, block))
        return carry

    zero = jnp.zeros((8, LANES), f32)
    norm = lax.fori_loop(0, 8, last_forward, (zero, zero))
    v0, v1, v2 = base[0], base[1], base[2]
    sums = dot_rows([(v0, v0), (v0, v1), (v0, v2), (v1, v1), (v1, v2), (v2, v2)], norm)
    z_out[0:8] = sums[0]
    z_out[8:16] = sums[1]
    each(1, devices, lambda k: z_copy(k).start())
    z_in[dim] = z_out[...]
    join(2, extract(sweep(), fold))
    each(0, devices, lambda k: unless(k == dim, lambda: z_arrival(k).wait_recv()))
    sums = tree([(z_in[k, 0:8], z_in[k, 8:16]) for k in range(devices)])
    s_out[0:8] = sums[0]
    s_out[8:16] = sums[1]
    each(1, 16, lambda k: s_copy(k).start())
    s_in[dp] = s_out[...]
    joined(2)

    @pl.when(owned)
    def _():
        each(1, 16, lambda k: ag_copy(1, k).start())
        last_in[slot] = base[3]

    each(0, 16, lambda k: unless(k == dp, lambda: s_arrival(k).wait_recv()))
    c0, c1, c2 = solve(tree([(s_in[k, 0:8], s_in[k, 8:16]) for k in range(16)]), scale)
    one = (jnp.ones_like(c0[0]), jnp.zeros_like(c0[0]))
    q0 = minus(one, scaled(c0, SHIFT))[0]
    q1 = -plus(c0, scaled(c1, SHIFT))[0]
    q2 = -plus(c1, scaled(c2, SHIFT))[0]
    q3 = -c2[0]
    c0, c1, c2 = c0[0], c1[0], c2[0]

    def arrived(which, r):
        unless(jnp.logical_and(owned, r == slot), lambda: ag_arrival(which, r).wait_recv())

    each(0, 8, lambda r: arrived(0, r))
    for d in range(8):
        for h in range(2):
            lanes = slice(h * LANES, (h + 1) * LANES)
            rows = pl.ds(d, 8, stride=8)
            v0, v1, v2 = [base_in[d, k, :, lanes] for k in range(3)]
            x_ref[h, rows, :] = books[h, rows, :] + (c0 * v0 + c1 * v1 + c2 * v2)
            base_in[d, 0, :, lanes] = q0 * v0 + q1 * v1 + q2 * v2
    each(0, 8, lambda r: arrived(1, r))
    for d in range(8):
        for h in range(2):
            lanes = slice(h * LANES, (h + 1) * LANES)
            r_ref[h, pl.ds(d, 8, stride=8), :] = base_in[d, 0, :, lanes] + q3 * last_in[d, :, lanes]

    each(1, 16, lambda k: ids_copy(k).wait_send())
    for other in range(2):
        each(0, 8, lambda d: pl.when(rs_away(d, other))(lambda: rs_copy(d, other).wait_send()))
    each(0, 3, lambda p: pair_copy(p).wait_send())
    each(1, devices, lambda k: z_copy(k).wait_send())
    each(1, 16, lambda k: s_copy(k).wait_send())

    @pl.when(owned)
    def _():
        each(1, 16, lambda k: ag_copy(0, k).wait_send())
        each(1, 16, lambda k: ag_copy(1, k).wait_send())


def per_device(planes, vectors, code_ids, start_books):
    sections, width, codes = start_books.shape
    count = code_ids.shape[1]
    scale = codes / (count * 16)
    devices = 2 * planes
    rows = sections * width
    books = jnp.transpose(start_books.reshape(rows, 2, LANES), (1, 0, 2))
    dma = pltpu.SemaphoreType.DMA
    halves = (2, rows, LANES)
    x, r = pl.pallas_call(
        functools.partial(kernel, planes, scale),
        out_shape=(jax.ShapeDtypeStruct(halves, f32),) * 2,
        in_specs=[pl.BlockSpec(memory_space=pl.ANY)] * 3,
        out_specs=(pl.BlockSpec(memory_space=pltpu.VMEM),) * 2,
        scratch_shapes=[
            pltpu.VMEM((width, count), f32),
            pltpu.VMEM(halves, f32),
            pltpu.VMEM((9, sections, count), jnp.int32),
            pltpu.VMEM((9, 64, count), bf16),
            pltpu.VMEM((9, count, CODES), bf16),
            pltpu.VMEM((width, count), f32),
            pltpu.VMEM((8, 1, count), f32),
            pltpu.VMEM((64, LANES), f32),
            pltpu.VMEM((128, CODES), f32),
            pltpu.VMEM((8, sections, CODES), f32),
            pltpu.VMEM((16, sections, CODES), f32),
            pltpu.VMEM((3, sections, CODES), f32),
            pltpu.VMEM((3, sections, CODES), f32),
            pltpu.VMEM((4, sections, CODES), f32),
            pltpu.VMEM((8, 3, sections, CODES), f32),
            pltpu.VMEM((8, sections, CODES), f32),
            pltpu.VMEM((16, LANES), f32),
            pltpu.VMEM((devices, 16, LANES), f32),
            pltpu.VMEM((16, LANES), f32),
            pltpu.VMEM((16, 16, LANES), f32),
            dma((3,)), dma((16,)), dma((8, 2)), dma((8, 2)), dma((16,)), dma((3,)), dma((3,)),
            dma((2, 16)), dma((2, 8)), dma((devices,)), dma((devices,)), dma((16,)), dma((16,)),
        ],
        compiler_params=pltpu.CompilerParams(
            collective_id=0, has_side_effects=True, vmem_limit_bytes=48 << 20
        ),
    )(vectors, code_ids, books)

    def back(array):
        return jnp.transpose(array, (1, 0, 2)).reshape(sections, width, codes)

    return back(x), back(r)


def solution(mesh):
    return jax.shard_map(
        functools.partial(per_device, mesh.shape["dim"] // 2),
        mesh=mesh,
        in_specs=(P("dim", "dp"), P(None, "dp"), P(None, "dim", None)),
        out_specs=(P(None, "dim", None), P(None, "dim", None)),
        check_vma=False,
    )
```

```python
import functools

import jax
import jax.numpy as jnp
from jax import lax
from jax.experimental import pallas as pl
from jax.experimental.pallas import tpu as pltpu
from jax.sharding import PartitionSpec as P

f32 = jnp.float32
bf16 = jnp.bfloat16
MESH = pl.DeviceIdType.MESH
LANES = 128
SECTIONS = 8
CODES = 256
RIDGE = 0.5
SHIFT = 2.0


def two_sum(a, b):
    s = a + b
    t = s - a
    return s, (a - (s - t)) + (b - t)


def two_prod(a, b):
    p = a * b
    ca = a * 4097.0
    ah = ca - (ca - a)
    al = a - ah
    cb = b * 4097.0
    bh = cb - (cb - b)
    bl = b - bh
    return p, ((ah * bh - p) + ah * bl + al * bh) + al * bl


def tidy(h, r):
    s = h + r
    return s, r - (s - h)


def plus(a, b):
    s, e = two_sum(a[0], b[0])
    return tidy(s, e + (a[1] + b[1]))


def minus(a, b):
    return plus(a, (-b[0], -b[1]))


def times(a, b):
    p, e = two_prod(a[0], b[0])
    return tidy(p, e + (a[0] * b[1] + a[1] * b[0]))


def over(a, b):
    first = a[0] / b[0]
    rest = minus(a, times((first, jnp.zeros_like(first)), b))
    return tidy(first, rest[0] / b[0])


def scaled(a, power):
    return a[0] * power, a[1] * power


def pick(table, index):
    place = index & (LANES - 1)
    low = jnp.take_along_axis(table[0], place, axis=1)
    high = jnp.take_along_axis(table[1], place, axis=1)
    return jnp.where(index >= LANES, high, low)


def make_masks(ids_ref, low_ref, high_ref, chunk=1024):
    count = ids_ref.shape[1]
    row_low = lax.broadcasted_iota(jnp.int32, (64, chunk), 0) & 7
    row_high = lax.broadcasted_iota(jnp.int32, (CODES, chunk), 0) & 31

    def step(k, carry):
        span = pl.ds(pl.multiple_of(k * chunk, chunk), chunk)
        code = ids_ref[:, span]
        top = code >> 5
        wide = jnp.concatenate(
            [jnp.broadcast_to(top[m : m + 1], (8, chunk)) for m in range(SECTIONS)], axis=0
        )
        low_ref[:, span] = jnp.where(wide == row_low, 1.0, 0.0).astype(bf16)
        part = code & 31
        wide = jnp.concatenate(
            [jnp.broadcast_to(part[m : m + 1], (32, chunk)) for m in range(SECTIONS)], axis=0
        )
        high_ref[span, :] = jnp.where(wide == row_high, 1.0, 0.0).astype(bf16).T
        return carry

    lax.fori_loop(0, count // chunk, step, 0)


def forward_local(books_ref, vec_ref, ids_ref, e_ref):
    count = ids_ref.shape[1]

    def step(g, carry):
        span = pl.ds(pl.multiple_of(g * LANES, LANES), LANES)
        code = ids_ref[:, span]
        total = vec_ref[:, span]
        for m in range(SECTIONS):
            total = total - pick(
                (books_ref[0, 8 * m : 8 * m + 8, :], books_ref[1, 8 * m : 8 * m + 8, :]), jnp.broadcast_to(code[m : m + 1], (8, LANES))
            )
        e_ref[:, span] = total
        return carry

    lax.fori_loop(0, count // LANES, step, 0, unroll=4)


def forward(table, ids_ref, e_ref, packed=False):
    count = ids_ref.shape[1]
    row = lax.broadcasted_iota(jnp.int32, (8, LANES), 0)
    blocks = []
    table = (table[:, :LANES], table[:, LANES:])
    for g in range(count // LANES):
        span = slice(g * LANES, (g + 1) * LANES)
        e = jnp.sum(pick(table, ids_ref[:, span]), axis=0, keepdims=True)
        e_ref[:, span] = e
        if packed:
            wide = jnp.broadcast_to(e, (8, LANES))
            if g % 8 == 0:
                blocks.append(wide)
            else:
                blocks[-1] = jnp.where(row == g % 8, wide, blocks[-1])
    return blocks


def weighted(low, e_row):
    wide = jnp.broadcast_to(e_row, (16, e_row.shape[1]))
    first = wide.astype(bf16)
    second = (wide - first.astype(f32)).astype(bf16)
    return jnp.concatenate(
        [low * jnp.concatenate([first] * 4, axis=0), low * jnp.concatenate([second] * 4, axis=0)],
        axis=0,
    )


def backward(low_ref, high_ref, e_ref, size=2048):
    total = None
    for q in range(low_ref.shape[1] // size):
        span = slice(q * size, (q + 1) * size)
        rows = weighted(low_ref[:, span], e_ref[:, span])
        term = jnp.dot(rows, high_ref[span, :], preferred_element_type=f32)
        total = term if total is None else total + term
    return total


def extract(acc, fold_ref):
    both = acc[:64] + acc[64:]
    for m in range(SECTIONS):
        half = both[8 * m : 8 * m + 8, :LANES] if m < 4 else both[8 * m : 8 * m + 8, LANES:]
        fold_ref[8 * m : 8 * m + 8, :] = half if m % 4 == 0 else pltpu.roll(half, LANES - 32 * (m % 4), 1)
    block = lax.broadcasted_iota(jnp.int32, (8, LANES), 1) >> 5
    halves = []
    for h in range(2):
        out = None
        for q in range(4):
            piece = fold_ref[pl.ds(4 * h + q, 8, stride=8), :]
            out = piece if q == 0 else jnp.where(block == q, pltpu.roll(piece, 32 * q, 1), out)
        halves.append(out)
    return jnp.concatenate(halves, axis=1)


def dot_rows(pairs, extra):
    row = lax.broadcasted_iota(jnp.int32, (8, LANES), 0)
    found = []
    for a, b in pairs:
        left = two_prod(a[:, :LANES], b[:, :LANES])
        right = two_prod(a[:, LANES:], b[:, LANES:])
        found.append(scaled(plus(left, right), 0.5))
    found.append(extra)
    high = jnp.zeros((8, LANES), f32)
    rest = jnp.zeros((8, LANES), f32)
    for q, pair in enumerate(found):
        for distance in (4, 2, 1):
            pair = plus(pair, (pltpu.roll(pair[0], distance, 0), pltpu.roll(pair[1], distance, 0)))
        high = jnp.where(row == q, pair[0], high)
        rest = jnp.where(row == q, pair[1], rest)
    pair = (high, rest)
    for distance in (64, 32, 16, 8, 4, 2, 1):
        pair = plus(pair, (pltpu.roll(pair[0], distance, 1), pltpu.roll(pair[1], distance, 1)))
    return pair


def tree(terms):
    while len(terms) > 1:
        terms = [plus(terms[k], terms[k + 1]) for k in range(0, len(terms), 2)]
    return terms[0]


def solve(total, scale):
    d00, d01, d02, d11, d12, d22, norm = [(total[0][q : q + 1], total[1][q : q + 1]) for q in range(7)]
    w00 = plus(d01, scaled(d00, SHIFT))
    w01 = plus(d02, scaled(d01, SHIFT))
    w02 = plus(d12, scaled(d02, SHIFT))
    w11 = plus(d12, scaled(d11, SHIFT))
    w12 = plus(d22, scaled(d12, SHIFT))
    w22 = plus(scaled(norm, scale), scaled(d22, RIDGE))
    l1 = over(w01, w00)
    l2 = over(w02, w00)
    p1 = minus(w11, times(l1, w01))
    u12 = minus(w12, times(l2, w01))
    l3 = over(u12, p1)
    p2 = minus(minus(w22, times(l2, w02)), times(l3, u12))
    y1 = minus(d01, times(l1, d00))
    y2 = minus(minus(d02, times(l2, d00)), times(l3, y1))
    c2 = over(y2, p2)
    c1 = minus(over(y1, p1), times(l3, c2))
    c0 = minus(minus(over(d00, w00), times(l1, c1)), times(l2, c2))
    return c0, c1, c2


def kernel(
    planes, scale, vec_hbm, ids_hbm, books_hbm, x_hbm, r_hbm,
    vec, books, ids, low, high, e_local, e_rows, e_even, e_odd, fold,
    rs_out, rs_in, pair_out, pair_in, base, base_in, last_in, x_out, r_out,
    z_out, z_in, s_out, s_in,
    in_sem, out_sem, ids_send, ids_recv, rs_send, rs_recv, pair_send, pair_recv,
    ag_send, ag_recv, z_send, z_recv, s_send, s_recv,
):
    dp = lax.axis_index("dp")
    dim = lax.axis_index("dim")
    core = dim % 2
    plane = dim // 2
    owner = dp // 8
    slot = dp % 8
    owned = core == owner
    half = ids.shape[2] // 2
    devices = 2 * planes

    def remote(src, dst, send_sem, recv_sem, target):
        return pltpu.make_async_remote_copy(
            src_ref=src, dst_ref=dst, send_sem=send_sem, recv_sem=recv_sem,
            device_id=target, device_id_type=MESH,
        )

    inputs = [
        pltpu.make_async_copy(ids_hbm, ids.at[8], in_sem.at[0]),
        pltpu.make_async_copy(vec_hbm, vec, in_sem.at[1]),
        pltpu.make_async_copy(books_hbm.at[:, 0:LANES], books.at[0], in_sem.at[2]),
        pltpu.make_async_copy(books_hbm.at[:, LANES:], books.at[1], in_sem.at[3]),
    ]
    for copy in inputs:
        copy.start()

    barrier = pltpu.get_barrier_semaphore()

    def greet_plane(k, carry):
        target = ((dp + k // 2) % 16, 2 * plane + (core + k) % 2)
        pl.semaphore_signal(barrier, inc=1, device_id=target, device_id_type=MESH)
        return carry

    def greet_line(k, carry):
        target = (dp, 2 * ((plane + k // 2) % planes) + k % 2)
        pl.semaphore_signal(barrier, inc=1, device_id=target, device_id_type=MESH)
        return carry

    lax.fori_loop(1, 32, greet_plane, 0)
    lax.fori_loop(2, devices, greet_line, 0)

    def ids_part(where, which):
        return ids.at[where, :, pl.ds(pl.multiple_of(which * half, half), half)]

    def ids_copy(k):
        return remote(
            ids_part(8, core), ids_part(slot, core), ids_send.at[k], ids_recv.at[slot, core],
            ((dp + k) % 16, 2 * plane + owner),
        )

    def ids_arrival(where, which):
        return remote(
            ids_part(8, which), ids_part(where, which), ids_send.at[0], ids_recv.at[where, which],
            (dp, 2 * plane + 1 - core),
        )

    def rs_copy(d, other):
        return remote(
            rs_out.at[d], rs_in.at[dp], rs_send.at[d, other], rs_recv.at[dp],
            (8 * core + d, 2 * plane + other),
        )

    def rs_away(d, other):
        return jnp.logical_or(8 * core + d != dp, other != core)

    def pair_copy(p):
        return remote(
            pair_out.at[p], pair_in.at[p], pair_send.at[p], pair_recv.at[p], (dp, 2 * plane + 1 - core)
        )

    def ag_copy(which, k):
        target = ((dp + k) % 16, dim)
        if which == 0:
            return remote(base.at[pl.ds(0, 3)], base_in.at[slot], ag_send.at[0, k], ag_recv.at[0, slot], target)
        return remote(base.at[3], last_in.at[slot], ag_send.at[1, k], ag_recv.at[1, slot], target)

    def ag_arrival(which, r):
        target = ((dp + 1) % 16, dim)
        if which == 0:
            return remote(base.at[pl.ds(0, 3)], base_in.at[r], ag_send.at[0, 0], ag_recv.at[0, r], target)
        return remote(base.at[3], last_in.at[r], ag_send.at[1, 0], ag_recv.at[1, r], target)

    def z_copy(k):
        return remote(z_out, z_in.at[dim], z_send.at[k], z_recv.at[dim], (dp, (dim + k) % devices))

    def z_arrival(k):
        return remote(z_out, z_in.at[k], z_send.at[0], z_recv.at[k], (dp, (dim + 1) % devices))

    def s_copy(k):
        return remote(s_out, s_in.at[dp], s_send.at[k], s_recv.at[dp], ((dp + k) % 16, dim))

    def s_arrival(k):
        return remote(s_out, s_in.at[k], s_send.at[0], s_recv.at[k], ((dp + 1) % 16, dim))

    def each(low_end, high_end, act):
        lax.fori_loop(low_end, high_end, lambda k, carry: (act(k), carry)[1], 0)

    def unless(skip, act):
        pl.when(jnp.logical_not(skip))(act)

    inputs[0].wait()
    pl.semaphore_wait(barrier, 31 + devices - 2)
    each(1, 16, lambda k: ids_copy(k).start())

    make_masks(ids.at[8], low.at[8], high.at[8])
    for copy in inputs[1:]:
        copy.wait()
    forward_local(books, vec, ids.at[8], e_local)
    for d in range(8):
        e_rows[d] = e_local[d : d + 1, :]
        for h in range(2):
            rs_out[d, :, h * LANES : (h + 1) * LANES] = (RIDGE / 16) * books[h, pl.ds(d, 8, stride=8), :]

    def local_pass(k, carry):
        d = (slot + k) % 8
        found = extract(backward(low.at[8], high.at[8], e_rows.at[d]), fold)
        rs_out[d] = scale * found - rs_out[d]
        for other in range(2):
            pl.when(rs_away(d, other))(lambda: rs_copy(d, other).start())
        return carry

    lax.fori_loop(0, 8, local_pass, 0)

    def place(q):
        return jnp.where(owned, jnp.where(q == 0, 8, (slot + 8 - q) % 8), 7 - q)

    def arrival(q):
        where = place(q)

        @pl.when(where < 8)
        def _():
            ids_arrival(where, 0).wait_recv()
            ids_arrival(where, 1).wait_recv()
            make_masks(ids.at[where], low.at[where], high.at[where])

    each(0, 8, arrival)

    @pl.when(owned)
    def _():
        rs_in[dp] = rs_out[slot]

    each(0, 16, lambda k: unless(jnp.logical_and(owned, k == dp), lambda: remote(
        rs_out.at[0], rs_in.at[k], rs_send.at[0, 0], rs_recv.at[k], (dp, 2 * plane + 1 - core)).wait_recv()))
    terms = [rs_in[k] for k in range(16)]
    while len(terms) > 1:
        terms = [terms[k] + terms[k + 1] for k in range(0, len(terms), 2)]
    base[0] = terms[0]

    def join(p, found):
        pair_out[p] = scale * found
        pair_copy(p).start()

    def joined(p):
        pair_copy(p).wait_recv()
        base[p + 1] = (pair_out[p] + pair_in[p]) + (RIDGE - SHIFT) * base[p]

    def sweep():
        def two(q, total):
            first, second = place(2 * q), place(2 * q + 1)
            one = backward(low.at[first], high.at[first], e_rows.at[2 * q])
            other = backward(low.at[second], high.at[second], e_rows.at[2 * q + 1])
            return total + (one + other)

        return lax.fori_loop(0, 4, two, jnp.zeros((128, CODES), f32))

    def ahead(table, q, rows):
        for u in range(2):
            forward(table, ids.at[place(2 * q + u)], rows.at[u])

    def behind(q, rows):
        terms = []
        for u in range(2):
            where = place(2 * q + u)
            terms.append(backward(low.at[where], high.at[where], rows.at[u]))
        return terms[0] + terms[1]

    def fused(table):
        ahead(table, 0, e_even)

        def four(t, total):
            total = total + behind(2 * t, e_even)
            ahead(table, 2 * t + 1, e_odd)
            total = total + behind(2 * t + 1, e_odd)
            ahead(table, (2 * t + 2) % 4, e_even)
            return total

        return lax.fori_loop(0, 2, four, jnp.zeros((128, CODES), f32))

    def early_pass(p):
        join(p, extract(fused(base[p]), fold))
        joined(p)

    each(0, 2, early_pass)

    @pl.when(owned)
    def _():
        each(1, 16, lambda k: ag_copy(0, k).start())
        base_in[slot] = base[0:3]

    def last_forward(q, carry):
        blocks = forward(base[2], ids.at[place(q)], e_rows.at[q], packed=True)
        for block in blocks:
            carry = plus(carry, two_prod(block, block))
        return carry

    zero = jnp.zeros((8, LANES), f32)
    norm = lax.fori_loop(0, 8, last_forward, (zero, zero))
    v0, v1, v2 = base[0], base[1], base[2]
    sums = dot_rows([(v0, v0), (v0, v1), (v0, v2), (v1, v1), (v1, v2), (v2, v2)], norm)
    z_out[0:8] = sums[0]
    z_out[8:16] = sums[1]
    each(1, devices, lambda k: z_copy(k).start())
    z_in[dim] = z_out[...]
    join(2, extract(sweep(), fold))
    each(0, devices, lambda k: unless(k == dim, lambda: z_arrival(k).wait_recv()))
    sums = tree([(z_in[k, 0:8], z_in[k, 8:16]) for k in range(devices)])
    s_out[0:8] = sums[0]
    s_out[8:16] = sums[1]
    each(1, 16, lambda k: s_copy(k).start())
    s_in[dp] = s_out[...]
    joined(2)

    @pl.when(owned)
    def _():
        each(1, 16, lambda k: ag_copy(1, k).start())
        last_in[slot] = base[3]

    each(0, 16, lambda k: unless(k == dp, lambda: s_arrival(k).wait_recv()))
    c0, c1, c2 = solve(tree([(s_in[k, 0:8], s_in[k, 8:16]) for k in range(16)]), scale)
    one = (jnp.ones_like(c0[0]), jnp.zeros_like(c0[0]))
    q0 = minus(one, scaled(c0, SHIFT))[0]
    q1 = -plus(c0, scaled(c1, SHIFT))[0]
    q2 = -plus(c1, scaled(c2, SHIFT))[0]
    q3 = -c2[0]
    c0, c1, c2 = c0[0], c1[0], c2[0]

    def arrived(which, r):
        unless(jnp.logical_and(owned, r == slot), lambda: ag_arrival(which, r).wait_recv())

    each(0, 8, lambda r: arrived(0, r))
    for d in range(8):
        for h in range(2):
            lanes = slice(h * LANES, (h + 1) * LANES)
            rows = pl.ds(d, 8, stride=8)
            v0, v1, v2 = [base_in[d, k, :, lanes] for k in range(3)]
            x_out[h, rows, :] = books[h, rows, :] + (c0 * v0 + c1 * v1 + c2 * v2)
            base_in[d, 0, :, lanes] = q0 * v0 + q1 * v1 + q2 * v2
    def outgoing(which):
        source, target = ((x_out, x_hbm), (r_out, r_hbm))[which]
        return [
            pltpu.make_async_copy(
                source.at[h], target.at[:, h * LANES : (h + 1) * LANES], out_sem.at[2 * which + h]
            )
            for h in range(2)
        ]

    for copy in outgoing(0):
        copy.start()
    each(0, 8, lambda r: arrived(1, r))
    for d in range(8):
        for h in range(2):
            lanes = slice(h * LANES, (h + 1) * LANES)
            r_out[h, pl.ds(d, 8, stride=8), :] = base_in[d, 0, :, lanes] + q3 * last_in[d, :, lanes]

    for copy in outgoing(1):
        copy.start()

    each(1, 16, lambda k: ids_copy(k).wait_send())
    for other in range(2):
        each(0, 8, lambda d: pl.when(rs_away(d, other))(lambda: rs_copy(d, other).wait_send()))
    each(0, 3, lambda p: pair_copy(p).wait_send())
    each(1, devices, lambda k: z_copy(k).wait_send())
    each(1, 16, lambda k: s_copy(k).wait_send())

    @pl.when(owned)
    def _():
        each(1, 16, lambda k: ag_copy(0, k).wait_send())
        each(1, 16, lambda k: ag_copy(1, k).wait_send())

    for copy in outgoing(0) + outgoing(1):
        copy.wait()


def per_device(planes, vectors, code_ids, start_books):
    sections, width, codes = start_books.shape
    count = code_ids.shape[1]
    scale = codes / (count * 16)
    devices = 2 * planes
    rows = sections * width
    books = start_books.reshape(rows, codes)
    dma = pltpu.SemaphoreType.DMA
    flat = (rows, codes)
    halves = (2, rows, LANES)
    x, r = pl.pallas_call(
        functools.partial(kernel, planes, scale),
        out_shape=(jax.ShapeDtypeStruct(flat, f32),) * 2,
        in_specs=[pl.BlockSpec(memory_space=pl.ANY)] * 3,
        out_specs=(pl.BlockSpec(memory_space=pl.ANY),) * 2,
        scratch_shapes=[
            pltpu.VMEM((width, count), f32),
            pltpu.VMEM(halves, f32),
            pltpu.VMEM((9, sections, count), jnp.int32),
            pltpu.VMEM((9, 64, count), bf16),
            pltpu.VMEM((9, count, CODES), bf16),
            pltpu.VMEM((width, count), f32),
            pltpu.VMEM((8, 1, count), f32),
            pltpu.VMEM((2, 1, count), f32),
            pltpu.VMEM((2, 1, count), f32),
            pltpu.VMEM((64, LANES), f32),
            pltpu.VMEM((8, sections, CODES), f32),
            pltpu.VMEM((16, sections, CODES), f32),
            pltpu.VMEM((3, sections, CODES), f32),
            pltpu.VMEM((3, sections, CODES), f32),
            pltpu.VMEM((4, sections, CODES), f32),
            pltpu.VMEM((8, 3, sections, CODES), f32),
            pltpu.VMEM((8, sections, CODES), f32),
            pltpu.VMEM(halves, f32),
            pltpu.VMEM(halves, f32),
            pltpu.VMEM((16, LANES), f32),
            pltpu.VMEM((devices, 16, LANES), f32),
            pltpu.VMEM((16, LANES), f32),
            pltpu.VMEM((16, 16, LANES), f32),
            dma((4,)), dma((4,)), dma((16,)), dma((8, 2)), dma((8, 2)), dma((16,)), dma((3,)), dma((3,)),
            dma((2, 16)), dma((2, 8)), dma((devices,)), dma((devices,)), dma((16,)), dma((16,)),
        ],
        compiler_params=pltpu.CompilerParams(
            collective_id=0, has_side_effects=True, vmem_limit_bytes=48 << 20
        ),
    )(vectors, code_ids, books)

    return x.reshape(sections, width, codes), r.reshape(sections, width, codes)


def solution(mesh):
    return jax.shard_map(
        functools.partial(per_device, mesh.shape["dim"] // 2),
        mesh=mesh,
        in_specs=(P("dim", "dp"), P(None, "dp"), P(None, "dim", None)),
        out_specs=(P(None, "dim", None), P(None, "dim", None)),
        check_vma=False,
    )
```

```python
import functools

import jax
import jax.numpy as jnp
from jax import lax
from jax.experimental import pallas as pl
from jax.experimental.pallas import tpu as pltpu
from jax.sharding import PartitionSpec as P

f32 = jnp.float32
bf16 = jnp.bfloat16
MESH = pl.DeviceIdType.MESH
LANES = 128
SECTIONS = 8
CODES = 256
RIDGE = 0.5
SHIFT = 2.0
EVEN = ((0, 0), (1, 1), (3, 3), (1, 3), (3, 1), (0, 2), (2, 0), (2, 2))
ODD = ((0, 1), (0, 3), (1, 0), (3, 0), (2, 1), (2, 3), (1, 2), (3, 2))
MOVES = tuple(move for pair in zip(ODD, EVEN[1:]) for move in pair) + (ODD[7],)
EARLY = 6


def entry(table, k, which):
    out = jnp.int32(table[0][which])
    for place in range(1, len(table)):
        out = jnp.where(k == place, table[place][which], out)
    return out


def two_sum(a, b):
    s = a + b
    t = s - a
    return s, (a - (s - t)) + (b - t)


def two_prod(a, b):
    p = a * b
    ca = a * 4097.0
    ah = ca - (ca - a)
    al = a - ah
    cb = b * 4097.0
    bh = cb - (cb - b)
    bl = b - bh
    return p, ((ah * bh - p) + ah * bl + al * bh) + al * bl


def tidy(h, r):
    s = h + r
    return s, r - (s - h)


def plus(a, b):
    s, e = two_sum(a[0], b[0])
    return tidy(s, e + (a[1] + b[1]))


def minus(a, b):
    return plus(a, (-b[0], -b[1]))


def times(a, b):
    p, e = two_prod(a[0], b[0])
    return tidy(p, e + (a[0] * b[1] + a[1] * b[0]))


def over(a, b):
    first = a[0] / b[0]
    rest = minus(a, times((first, jnp.zeros_like(first)), b))
    return tidy(first, rest[0] / b[0])


def scaled(a, power):
    return a[0] * power, a[1] * power


def pick(table, index):
    place = index & (LANES - 1)
    low = jnp.take_along_axis(table[0], place, axis=1)
    high = jnp.take_along_axis(table[1], place, axis=1)
    return jnp.where(index >= LANES, high, low)


def make_masks(ids_ref, low_ref, high_ref, chunk=1024):
    count = ids_ref.shape[1]
    row_low = lax.broadcasted_iota(jnp.int32, (64, chunk), 0) & 7
    row_high = lax.broadcasted_iota(jnp.int32, (CODES, chunk), 0) & 31

    def step(k, carry):
        span = pl.ds(pl.multiple_of(k * chunk, chunk), chunk)
        code = ids_ref[:, span]
        top = code >> 5
        wide = jnp.concatenate(
            [jnp.broadcast_to(top[m : m + 1], (8, chunk)) for m in range(SECTIONS)], axis=0
        )
        low_ref[:, span] = jnp.where(wide == row_low, 1.0, 0.0).astype(bf16)
        part = code & 31
        wide = jnp.concatenate(
            [jnp.broadcast_to(part[m : m + 1], (32, chunk)) for m in range(SECTIONS)], axis=0
        )
        high_ref[span, :] = jnp.where(wide == row_high, 1.0, 0.0).astype(bf16).T
        return carry

    lax.fori_loop(0, count // chunk, step, 0)


def forward_local(books_ref, vec_ref, ids_ref, e_ref):
    count = ids_ref.shape[1]

    def step(g, carry):
        span = pl.ds(pl.multiple_of(g * LANES, LANES), LANES)
        code = ids_ref[:, span]
        total = vec_ref[:, span]
        for m in range(SECTIONS):
            total = total - pick(
                (books_ref[0, 8 * m : 8 * m + 8, :], books_ref[1, 8 * m : 8 * m + 8, :]), jnp.broadcast_to(code[m : m + 1], (8, LANES))
            )
        e_ref[:, span] = total
        return carry

    lax.fori_loop(0, count // LANES, step, 0, unroll=4)


def forward(table, ids_ref, e_ref, packed=False):
    count = ids_ref.shape[1]
    row = lax.broadcasted_iota(jnp.int32, (8, LANES), 0)
    blocks = []
    table = (table[:, :LANES], table[:, LANES:])
    for g in range(count // LANES):
        span = slice(g * LANES, (g + 1) * LANES)
        e = jnp.sum(pick(table, ids_ref[:, span]), axis=0, keepdims=True)
        e_ref[:, span] = e
        if packed:
            wide = jnp.broadcast_to(e, (8, LANES))
            if g % 8 == 0:
                blocks.append(wide)
            else:
                blocks[-1] = jnp.where(row == g % 8, wide, blocks[-1])
    return blocks


def weighted(low, e_row):
    wide = jnp.broadcast_to(e_row, (16, e_row.shape[1]))
    first = wide.astype(bf16)
    second = (wide - first.astype(f32)).astype(bf16)
    return jnp.concatenate(
        [low * jnp.concatenate([first] * 4, axis=0), low * jnp.concatenate([second] * 4, axis=0)],
        axis=0,
    )


def backward(low_ref, high_ref, e_ref, size=2048):
    total = None
    for q in range(low_ref.shape[1] // size):
        span = slice(q * size, (q + 1) * size)
        rows = weighted(low_ref[:, span], e_ref[:, span])
        term = jnp.dot(rows, high_ref[span, :], preferred_element_type=f32)
        total = term if total is None else total + term
    return total


def extract(acc, fold_ref):
    both = acc[:64] + acc[64:]
    for m in range(SECTIONS):
        half = both[8 * m : 8 * m + 8, :LANES] if m < 4 else both[8 * m : 8 * m + 8, LANES:]
        fold_ref[8 * m : 8 * m + 8, :] = half if m % 4 == 0 else pltpu.roll(half, LANES - 32 * (m % 4), 1)
    block = lax.broadcasted_iota(jnp.int32, (8, LANES), 1) >> 5
    halves = []
    for h in range(2):
        out = None
        for q in range(4):
            piece = fold_ref[pl.ds(4 * h + q, 8, stride=8), :]
            out = piece if q == 0 else jnp.where(block == q, pltpu.roll(piece, 32 * q, 1), out)
        halves.append(out)
    return jnp.concatenate(halves, axis=1)


def dot_rows(pairs, extra):
    row = lax.broadcasted_iota(jnp.int32, (8, LANES), 0)
    found = []
    for a, b in pairs:
        left = two_prod(a[:, :LANES], b[:, :LANES])
        right = two_prod(a[:, LANES:], b[:, LANES:])
        found.append(scaled(plus(left, right), 0.5))
    found.append(extra)
    high = jnp.zeros((8, LANES), f32)
    rest = jnp.zeros((8, LANES), f32)
    for q, pair in enumerate(found):
        for distance in (4, 2, 1):
            pair = plus(pair, (pltpu.roll(pair[0], distance, 0), pltpu.roll(pair[1], distance, 0)))
        high = jnp.where(row == q, pair[0], high)
        rest = jnp.where(row == q, pair[1], rest)
    pair = (high, rest)
    for distance in (64, 32, 16, 8, 4, 2, 1):
        pair = plus(pair, (pltpu.roll(pair[0], distance, 1), pltpu.roll(pair[1], distance, 1)))
    return pair


def tree(terms):
    while len(terms) > 1:
        terms = [plus(terms[k], terms[k + 1]) for k in range(0, len(terms), 2)]
    return terms[0]


def solve(total, scale):
    d00, d01, d02, d11, d12, d22, norm = [(total[0][q : q + 1], total[1][q : q + 1]) for q in range(7)]
    w00 = plus(d01, scaled(d00, SHIFT))
    w01 = plus(d02, scaled(d01, SHIFT))
    w02 = plus(d12, scaled(d02, SHIFT))
    w11 = plus(d12, scaled(d11, SHIFT))
    w12 = plus(d22, scaled(d12, SHIFT))
    w22 = plus(scaled(norm, scale), scaled(d22, RIDGE))
    l1 = over(w01, w00)
    l2 = over(w02, w00)
    p1 = minus(w11, times(l1, w01))
    u12 = minus(w12, times(l2, w01))
    l3 = over(u12, p1)
    p2 = minus(minus(w22, times(l2, w02)), times(l3, u12))
    y1 = minus(d01, times(l1, d00))
    y2 = minus(minus(d02, times(l2, d00)), times(l3, y1))
    c2 = over(y2, p2)
    c1 = minus(over(y1, p1), times(l3, c2))
    c0 = minus(minus(over(d00, w00), times(l1, c1)), times(l2, c2))
    return c0, c1, c2


def kernel(
    planes, scale, vec_hbm, ids_hbm, books_hbm, x_hbm, r_hbm,
    vec, books, ids, low, high, e_local, e_rows, e_even, e_odd, fold,
    rs_out, rs_in, pair_out, pair_in, base, base_in, last_in, x_out, r_out,
    z_out, z_in, s_out, s_in,
    in_sem, out_sem, ids_send, ids_recv, rs_send, rs_recv, pair_send, pair_recv,
    ag_send, ag_recv, z_send, z_recv, s_send, s_recv,
):
    dp = lax.axis_index("dp")
    dim = lax.axis_index("dim")
    core = dim % 2
    plane = dim // 2
    y, x = dp // 4, dp % 4
    owner, slot = dp // 8, dp % 8
    owned = core == owner
    keeper = (y + x) % 2
    kept = core == keeper
    half = ids.shape[2] // 2
    devices = 2 * planes

    def remote(src, dst, send_sem, recv_sem, target):
        return pltpu.make_async_remote_copy(
            src_ref=src, dst_ref=dst, send_sem=send_sem, recv_sem=recv_sem,
            device_id=target, device_id_type=MESH,
        )

    inputs = [
        pltpu.make_async_copy(ids_hbm, ids.at[8], in_sem.at[0]),
        pltpu.make_async_copy(vec_hbm, vec, in_sem.at[1]),
        pltpu.make_async_copy(books_hbm.at[:, 0:LANES], books.at[0], in_sem.at[2]),
        pltpu.make_async_copy(books_hbm.at[:, LANES:], books.at[1], in_sem.at[3]),
    ]
    for copy in inputs:
        copy.start()

    barrier = pltpu.get_barrier_semaphore()

    def greet_plane(k, carry):
        target = ((dp + k // 2) % 16, 2 * plane + (core + k) % 2)
        pl.semaphore_signal(barrier, inc=1, device_id=target, device_id_type=MESH)
        return carry

    def greet_line(k, carry):
        target = (dp, 2 * ((plane + k // 2) % planes) + k % 2)
        pl.semaphore_signal(barrier, inc=1, device_id=target, device_id_type=MESH)
        return carry

    lax.fori_loop(1, 32, greet_plane, 0)
    lax.fori_loop(2, devices, greet_line, 0)

    def ids_part(where, which):
        return ids.at[where, :, pl.ds(pl.multiple_of(which * half, half), half)]

    def ids_copy(k):
        return remote(
            ids_part(8, core), ids_part((k + 1) // 2, core), ids_send.at[k], ids_recv.at[(k + 1) // 2, core],
            ((y + entry(MOVES, k, 0)) % 4 * 4 + (x + entry(MOVES, k, 1)) % 4, 2 * plane + keeper),
        )

    def ids_arrival(where, which):
        return remote(
            ids_part(8, which), ids_part(where, which), ids_send.at[0], ids_recv.at[where, which],
            (dp, 2 * plane + 1 - core),
        )

    def rs_copy(d, other):
        return remote(
            rs_out.at[d], rs_in.at[dp], rs_send.at[d, other], rs_recv.at[dp],
            (8 * core + d, 2 * plane + other),
        )

    def rs_away(d, other):
        return jnp.logical_or(8 * core + d != dp, other != core)

    def pair_copy(p):
        return remote(
            pair_out.at[p], pair_in.at[p], pair_send.at[p], pair_recv.at[p], (dp, 2 * plane + 1 - core)
        )

    def ag_copy(which, k):
        target = ((dp + k) % 16, dim)
        if which == 0:
            return remote(base.at[pl.ds(0, 3)], base_in.at[slot], ag_send.at[0, k], ag_recv.at[0, slot], target)
        return remote(base.at[3], last_in.at[slot], ag_send.at[1, k], ag_recv.at[1, slot], target)

    def ag_arrival(which, r):
        target = ((dp + 1) % 16, dim)
        if which == 0:
            return remote(base.at[pl.ds(0, 3)], base_in.at[r], ag_send.at[0, 0], ag_recv.at[0, r], target)
        return remote(base.at[3], last_in.at[r], ag_send.at[1, 0], ag_recv.at[1, r], target)

    def z_copy(k):
        return remote(z_out, z_in.at[dim], z_send.at[k], z_recv.at[dim], (dp, (dim + k) % devices))

    def z_arrival(k):
        return remote(z_out, z_in.at[k], z_send.at[0], z_recv.at[k], (dp, (dim + 1) % devices))

    def s_copy(k):
        return remote(s_out, s_in.at[dp], s_send.at[k], s_recv.at[dp], ((dp + k) % 16, dim))

    def s_arrival(k):
        return remote(s_out, s_in.at[k], s_send.at[0], s_recv.at[k], ((dp + 1) % 16, dim))

    def each(low_end, high_end, act):
        lax.fori_loop(low_end, high_end, lambda k, carry: (act(k), carry)[1], 0)

    def unless(skip, act):
        pl.when(jnp.logical_not(skip))(act)

    inputs[0].wait()
    pl.semaphore_wait(barrier, 31 + devices - 2)
    each(0, 5, lambda k: ids_copy(k).start())

    make_masks(ids.at[8], low.at[8], high.at[8])
    for copy in inputs[1:]:
        copy.wait()
    forward_local(books, vec, ids.at[8], e_local)
    for d in range(8):
        e_rows[d] = e_local[d : d + 1, :]
        for h in range(2):
            rs_out[d, :, h * LANES : (h + 1) * LANES] = (RIDGE / 16) * books[h, pl.ds(d, 8, stride=8), :]

    each(5, 7, lambda k: ids_copy(k).start())

    def local_pass(k, carry):
        d = (slot + k) % 8
        found = extract(backward(low.at[8], high.at[8], e_rows.at[d]), fold)
        rs_out[d] = scale * found - rs_out[d]
        for other in range(2):
            pl.when(rs_away(d, other))(lambda: rs_copy(d, other).start())
        ids_copy(7 + k).start()
        return carry

    lax.fori_loop(0, 8, local_pass, 0)

    def place(q):
        return jnp.where(jnp.logical_and(kept, q == 0), 8, q)

    def arrival(q):
        where = place(q)

        @pl.when(where < 8)
        def _():
            ids_arrival(where, 0).wait_recv()
            ids_arrival(where, 1).wait_recv()
            make_masks(ids.at[where], low.at[where], high.at[where])

    each(0, EARLY, arrival)

    @pl.when(owned)
    def _():
        rs_in[dp] = rs_out[slot]

    each(0, 16, lambda k: unless(jnp.logical_and(owned, k == dp), lambda: remote(
        rs_out.at[0], rs_in.at[k], rs_send.at[0, 0], rs_recv.at[k], (dp, 2 * plane + 1 - core)).wait_recv()))
    terms = [rs_in[k] for k in range(16)]
    while len(terms) > 1:
        terms = [terms[k] + terms[k + 1] for k in range(0, len(terms), 2)]
    base[0] = terms[0]

    def join(p, found):
        pair_out[p] = scale * found
        pair_copy(p).start()

    def joined(p):
        pair_copy(p).wait_recv()
        base[p + 1] = (pair_out[p] + pair_in[p]) + (RIDGE - SHIFT) * base[p]

    def sweep():
        def two(q, total):
            first, second = place(2 * q), place(2 * q + 1)
            one = backward(low.at[first], high.at[first], e_rows.at[2 * q])
            other = backward(low.at[second], high.at[second], e_rows.at[2 * q + 1])
            return total + (one + other)

        return lax.fori_loop(0, 4, two, jnp.zeros((128, CODES), f32))

    def ahead(table, q, rows):
        for u in range(2):
            forward(table, ids.at[place(2 * q + u)], rows.at[u])

    def behind(q, rows):
        terms = []
        for u in range(2):
            where = place(2 * q + u)
            terms.append(backward(low.at[where], high.at[where], rows.at[u]))
        return terms[0] + terms[1]

    def fused(table):
        ahead(table, 0, e_even)

        def four(t, total):
            total = total + behind(2 * t, e_even)
            ahead(table, 2 * t + 1, e_odd)
            total = total + behind(2 * t + 1, e_odd)
            ahead(table, (2 * t + 2) % 4, e_even)
            return total

        return lax.fori_loop(0, 2, four, jnp.zeros((128, CODES), f32))

    def first(t, total):
        @pl.when(2 * t >= EARLY)
        def _():
            arrival(2 * t)
            arrival(2 * t + 1)

        ahead(base[0], t, e_even)
        return total + behind(t, e_even)

    join(0, extract(lax.fori_loop(0, 4, first, jnp.zeros((128, CODES), f32)), fold))
    joined(0)
    join(1, extract(fused(base[1]), fold))
    joined(1)

    @pl.when(owned)
    def _():
        each(1, 16, lambda k: ag_copy(0, k).start())
        base_in[slot] = base[0:3]

    def last_forward(t, carry):
        blocks = []
        for q in (2 * t, 2 * t + 1):
            blocks += forward(base[2], ids.at[place(q)], e_rows.at[q], packed=True)
        return plus(carry, tree([two_prod(block, block) for block in blocks]))

    zero = jnp.zeros((8, LANES), f32)
    norm = lax.fori_loop(0, 4, last_forward, (zero, zero))
    v0, v1, v2 = base[0], base[1], base[2]
    sums = dot_rows([(v0, v0), (v0, v1), (v0, v2), (v1, v1), (v1, v2), (v2, v2)], norm)
    z_out[0:8] = sums[0]
    z_out[8:16] = sums[1]
    each(1, devices, lambda k: z_copy(k).start())
    z_in[dim] = z_out[...]
    join(2, extract(sweep(), fold))
    each(0, devices, lambda k: unless(k == dim, lambda: z_arrival(k).wait_recv()))
    sums = tree([(z_in[k, 0:8], z_in[k, 8:16]) for k in range(devices)])
    s_out[0:8] = sums[0]
    s_out[8:16] = sums[1]
    each(1, 16, lambda k: s_copy(k).start())
    s_in[dp] = s_out[...]
    joined(2)

    @pl.when(owned)
    def _():
        each(1, 16, lambda k: ag_copy(1, k).start())
        last_in[slot] = base[3]

    each(0, 16, lambda k: unless(k == dp, lambda: s_arrival(k).wait_recv()))
    c0, c1, c2 = solve(tree([(s_in[k, 0:8], s_in[k, 8:16]) for k in range(16)]), scale)
    one = (jnp.ones_like(c0[0]), jnp.zeros_like(c0[0]))
    q0 = minus(one, scaled(c0, SHIFT))[0]
    q1 = -plus(c0, scaled(c1, SHIFT))[0]
    q2 = -plus(c1, scaled(c2, SHIFT))[0]
    q3 = -c2[0]
    c0, c1, c2 = c0[0], c1[0], c2[0]

    def arrived(which, r):
        unless(jnp.logical_and(owned, r == slot), lambda: ag_arrival(which, r).wait_recv())

    each(0, 8, lambda r: arrived(0, r))
    for d in range(8):
        for h in range(2):
            lanes = slice(h * LANES, (h + 1) * LANES)
            rows = pl.ds(d, 8, stride=8)
            v0, v1, v2 = [base_in[d, k, :, lanes] for k in range(3)]
            x_out[h, rows, :] = books[h, rows, :] + (c0 * v0 + c1 * v1 + c2 * v2)
            base_in[d, 0, :, lanes] = q0 * v0 + q1 * v1 + q2 * v2
    def outgoing(which):
        source, target = ((x_out, x_hbm), (r_out, r_hbm))[which]
        return [
            pltpu.make_async_copy(
                source.at[h], target.at[:, h * LANES : (h + 1) * LANES], out_sem.at[2 * which + h]
            )
            for h in range(2)
        ]

    for copy in outgoing(0):
        copy.start()
    each(0, 8, lambda r: arrived(1, r))
    for d in range(8):
        for h in range(2):
            lanes = slice(h * LANES, (h + 1) * LANES)
            r_out[h, pl.ds(d, 8, stride=8), :] = base_in[d, 0, :, lanes] + q3 * last_in[d, :, lanes]

    for copy in outgoing(1):
        copy.start()

    each(0, 15, lambda k: ids_copy(k).wait_send())
    for other in range(2):
        each(0, 8, lambda d: pl.when(rs_away(d, other))(lambda: rs_copy(d, other).wait_send()))
    each(0, 3, lambda p: pair_copy(p).wait_send())
    each(1, devices, lambda k: z_copy(k).wait_send())
    each(1, 16, lambda k: s_copy(k).wait_send())

    @pl.when(owned)
    def _():
        each(1, 16, lambda k: ag_copy(0, k).wait_send())
        each(1, 16, lambda k: ag_copy(1, k).wait_send())

    for copy in outgoing(0) + outgoing(1):
        copy.wait()


def per_device(planes, vectors, code_ids, start_books):
    sections, width, codes = start_books.shape
    count = code_ids.shape[1]
    scale = codes / (count * 16)
    devices = 2 * planes
    rows = sections * width
    books = start_books.reshape(rows, codes)
    dma = pltpu.SemaphoreType.DMA
    flat = (rows, codes)
    halves = (2, rows, LANES)
    x, r = pl.pallas_call(
        functools.partial(kernel, planes, scale),
        out_shape=(jax.ShapeDtypeStruct(flat, f32),) * 2,
        in_specs=[pl.BlockSpec(memory_space=pl.ANY)] * 3,
        out_specs=(pl.BlockSpec(memory_space=pl.ANY),) * 2,
        scratch_shapes=[
            pltpu.VMEM((width, count), f32),
            pltpu.VMEM(halves, f32),
            pltpu.VMEM((9, sections, count), jnp.int32),
            pltpu.VMEM((9, 64, count), bf16),
            pltpu.VMEM((9, count, CODES), bf16),
            pltpu.VMEM((width, count), f32),
            pltpu.VMEM((8, 1, count), f32),
            pltpu.VMEM((2, 1, count), f32),
            pltpu.VMEM((2, 1, count), f32),
            pltpu.VMEM((64, LANES), f32),
            pltpu.VMEM((8, sections, CODES), f32),
            pltpu.VMEM((16, sections, CODES), f32),
            pltpu.VMEM((3, sections, CODES), f32),
            pltpu.VMEM((3, sections, CODES), f32),
            pltpu.VMEM((4, sections, CODES), f32),
            pltpu.VMEM((8, 3, sections, CODES), f32),
            pltpu.VMEM((8, sections, CODES), f32),
            pltpu.VMEM(halves, f32),
            pltpu.VMEM(halves, f32),
            pltpu.VMEM((16, LANES), f32),
            pltpu.VMEM((devices, 16, LANES), f32),
            pltpu.VMEM((16, LANES), f32),
            pltpu.VMEM((16, 16, LANES), f32),
            dma((4,)), dma((4,)), dma((16,)), dma((8, 2)), dma((8, 2)), dma((16,)), dma((3,)), dma((3,)),
            dma((2, 16)), dma((2, 8)), dma((devices,)), dma((devices,)), dma((16,)), dma((16,)),
        ],
        compiler_params=pltpu.CompilerParams(
            collective_id=0, has_side_effects=True, vmem_limit_bytes=61 << 20
        ),
    )(vectors, code_ids, books)

    return x.reshape(sections, width, codes), r.reshape(sections, width, codes)


def solution(mesh):
    return jax.shard_map(
        functools.partial(per_device, mesh.shape["dim"] // 2),
        mesh=mesh,
        in_specs=(P("dim", "dp"), P(None, "dp"), P(None, "dim", None)),
        out_specs=(P(None, "dim", None), P(None, "dim", None)),
        check_vma=False,
    )
```

```python
import functools

import jax
import jax.numpy as jnp
from jax import lax
from jax.experimental import pallas as pl
from jax.experimental.pallas import tpu as pltpu
from jax.sharding import PartitionSpec as P

f32 = jnp.float32
bf16 = jnp.bfloat16
MESH = pl.DeviceIdType.MESH
LANES = 128
SECTIONS = 8
CODES = 256
RIDGE = 0.5
SHIFT = 2.0
EVEN = ((0, 0), (1, 1), (3, 3), (1, 3), (3, 1), (0, 2), (2, 0), (2, 2))
ODD = ((0, 1), (0, 3), (1, 0), (3, 0), (2, 1), (2, 3), (1, 2), (3, 2))
MOVES = tuple(move for pair in zip(ODD, EVEN[1:]) for move in pair) + (ODD[7],)
EARLY = 6


def entry(table, k, which):
    if isinstance(k, int):
        return table[k][which]
    out = jnp.int32(table[0][which])
    for place in range(1, len(table)):
        out = jnp.where(k == place, table[place][which], out)
    return out


def two_sum(a, b):
    s = a + b
    t = s - a
    return s, (a - (s - t)) + (b - t)


def two_prod(a, b):
    p = a * b
    ca = a * 4097.0
    ah = ca - (ca - a)
    al = a - ah
    cb = b * 4097.0
    bh = cb - (cb - b)
    bl = b - bh
    return p, ((ah * bh - p) + ah * bl + al * bh) + al * bl


def tidy(h, r):
    s = h + r
    return s, r - (s - h)


def plus(a, b):
    s, e = two_sum(a[0], b[0])
    return tidy(s, e + (a[1] + b[1]))


def minus(a, b):
    return plus(a, (-b[0], -b[1]))


def times(a, b):
    p, e = two_prod(a[0], b[0])
    return tidy(p, e + (a[0] * b[1] + a[1] * b[0]))


def over(a, b):
    first = a[0] / b[0]
    rest = minus(a, times((first, jnp.zeros_like(first)), b))
    return tidy(first, rest[0] / b[0])


def scaled(a, power):
    return a[0] * power, a[1] * power


def pick(table, index):
    place = index & (LANES - 1)
    low = jnp.take_along_axis(table[0], place, axis=1)
    high = jnp.take_along_axis(table[1], place, axis=1)
    return jnp.where(index >= LANES, high, low)


def make_masks(ids_ref, low_ref, high_ref, chunk=2048):
    count = ids_ref.shape[1]
    row_low = lax.broadcasted_iota(jnp.int32, (64, chunk), 0) & 7
    row_high = lax.broadcasted_iota(jnp.int32, (CODES, chunk), 0) & 31

    def step(k, carry):
        span = pl.ds(pl.multiple_of(k * chunk, chunk), chunk)
        code = ids_ref[:, span]
        top = code >> 5
        wide = jnp.concatenate(
            [jnp.broadcast_to(top[m : m + 1], (8, chunk)) for m in range(SECTIONS)], axis=0
        )
        low_ref[:, span] = jnp.where(wide == row_low, 1.0, 0.0).astype(bf16)
        part = code & 31
        wide = jnp.concatenate(
            [jnp.broadcast_to(part[m : m + 1], (32, chunk)) for m in range(SECTIONS)], axis=0
        )
        high_ref[span, :] = jnp.where(wide == row_high, 1.0, 0.0).astype(bf16).T
        return carry

    lax.fori_loop(0, count // chunk, step, 0)


def forward_local(books_ref, vec_ref, ids_ref, e_ref):
    count = ids_ref.shape[1]

    def step(g, carry):
        span = pl.ds(pl.multiple_of(g * LANES, LANES), LANES)
        code = ids_ref[:, span]
        total = vec_ref[:, span]
        for m in range(SECTIONS):
            total = total - pick(
                (books_ref[0, 8 * m : 8 * m + 8, :], books_ref[1, 8 * m : 8 * m + 8, :]), jnp.broadcast_to(code[m : m + 1], (8, LANES))
            )
        e_ref[:, span] = total
        return carry

    lax.fori_loop(0, count // LANES, step, 0, unroll=8)


def forward(table, ids_ref, e_ref, packed=False):
    count = ids_ref.shape[1]
    row = lax.broadcasted_iota(jnp.int32, (8, LANES), 0)
    blocks = []
    table = (table[:, :LANES], table[:, LANES:])
    for g in range(count // LANES):
        span = slice(g * LANES, (g + 1) * LANES)
        e = jnp.sum(pick(table, ids_ref[:, span]), axis=0, keepdims=True)
        e_ref[:, span] = e
        if packed:
            wide = jnp.broadcast_to(e, (8, LANES))
            if g % 8 == 0:
                blocks.append(wide)
            else:
                blocks[-1] = jnp.where(row == g % 8, wide, blocks[-1])
    return blocks


def weighted(low, e_row):
    wide = jnp.broadcast_to(e_row, (16, e_row.shape[1]))
    first = wide.astype(bf16)
    second = (wide - first.astype(f32)).astype(bf16)
    return jnp.concatenate(
        [low * jnp.concatenate([first] * 4, axis=0), low * jnp.concatenate([second] * 4, axis=0)],
        axis=0,
    )


def backward(low_ref, high_ref, e_ref, size=2048):
    total = None
    for q in range(low_ref.shape[1] // size):
        span = slice(q * size, (q + 1) * size)
        rows = weighted(low_ref[:, span], e_ref[:, span])
        term = jnp.dot(rows, high_ref[span, :], preferred_element_type=f32)
        total = term if total is None else total + term
    return total


def extract(acc, fold_ref):
    both = acc[:64] + acc[64:]
    for m in range(SECTIONS):
        half = both[8 * m : 8 * m + 8, :LANES] if m < 4 else both[8 * m : 8 * m + 8, LANES:]
        fold_ref[8 * m : 8 * m + 8, :] = half if m % 4 == 0 else pltpu.roll(half, LANES - 32 * (m % 4), 1)
    block = lax.broadcasted_iota(jnp.int32, (8, LANES), 1) >> 5
    halves = []
    for h in range(2):
        out = None
        for q in range(4):
            piece = fold_ref[pl.ds(4 * h + q, 8, stride=8), :]
            out = piece if q == 0 else jnp.where(block == q, pltpu.roll(piece, 32 * q, 1), out)
        halves.append(out)
    return jnp.concatenate(halves, axis=1)


def dots(pairs, first, carry, extra=()):
    row = lax.broadcasted_iota(jnp.int32, (8, LANES), 0)
    found = []
    for a, b in pairs:
        left = two_prod(a[:, :LANES], b[:, :LANES])
        right = two_prod(a[:, LANES:], b[:, LANES:])
        found.append(scaled(plus(left, right), 0.5))
    high, rest = carry
    for q, pair in enumerate(found + list(extra)):
        for distance in (4, 2, 1):
            pair = plus(pair, (pltpu.roll(pair[0], distance, 0), pltpu.roll(pair[1], distance, 0)))
        high = jnp.where(row == first + q, pair[0], high)
        rest = jnp.where(row == first + q, pair[1], rest)
    return high, rest


def over_lanes(pair):
    for distance in (64, 32, 16, 8, 4, 2, 1):
        pair = plus(pair, (pltpu.roll(pair[0], distance, 1), pltpu.roll(pair[1], distance, 1)))
    return pair


def tree(terms):
    while len(terms) > 1:
        terms = [plus(terms[k], terms[k + 1]) for k in range(0, len(terms), 2)]
    return terms[0]


def solve(total, scale):
    d00, d01, d11, d02, d12, d22, norm = [(total[0][q : q + 1], total[1][q : q + 1]) for q in range(7)]
    w00 = plus(d01, scaled(d00, SHIFT))
    w01 = plus(d02, scaled(d01, SHIFT))
    w02 = plus(d12, scaled(d02, SHIFT))
    w11 = plus(d12, scaled(d11, SHIFT))
    w12 = plus(d22, scaled(d12, SHIFT))
    w22 = plus(scaled(norm, scale), scaled(d22, RIDGE))
    l1 = over(w01, w00)
    l2 = over(w02, w00)
    p1 = minus(w11, times(l1, w01))
    u12 = minus(w12, times(l2, w01))
    l3 = over(u12, p1)
    p2 = minus(minus(w22, times(l2, w02)), times(l3, u12))
    y1 = minus(d01, times(l1, d00))
    y2 = minus(minus(d02, times(l2, d00)), times(l3, y1))
    c2 = over(y2, p2)
    c1 = minus(over(y1, p1), times(l3, c2))
    c0 = minus(minus(over(d00, w00), times(l1, c1)), times(l2, c2))
    return c0, c1, c2


def kernel(
    planes, scale, vec_hbm, ids_hbm, books_hbm, x_hbm, r_hbm,
    vec, books, ids, low, high, e_local, e_rows, e_even, e_odd, fold,
    rs_out, rs_in, pair_out, pair_in, base, base_in, last_in, x_out, r_out,
    z_out, z_in, s_out, s_in,
    in_sem, out_sem, ids_send, ids_recv, rs_send, rs_recv, pair_send, pair_recv,
    ag_send, ag_recv, z_send, z_recv, s_send, s_recv,
):
    dp = lax.axis_index("dp")
    dim = lax.axis_index("dim")
    core = dim % 2
    plane = dim // 2
    y, x = dp // 4, dp % 4
    owner, slot = dp // 8, dp % 8
    owned = core == owner
    keeper = (y + x) % 2
    kept = core == keeper
    half = ids.shape[2] // 2
    devices = 2 * planes

    def remote(src, dst, send_sem, recv_sem, target):
        return pltpu.make_async_remote_copy(
            src_ref=src, dst_ref=dst, send_sem=send_sem, recv_sem=recv_sem,
            device_id=target, device_id_type=MESH,
        )

    inputs = [
        pltpu.make_async_copy(ids_hbm, ids.at[8], in_sem.at[0]),
        pltpu.make_async_copy(vec_hbm, vec, in_sem.at[1]),
        pltpu.make_async_copy(books_hbm.at[:, 0:LANES], books.at[0], in_sem.at[2]),
        pltpu.make_async_copy(books_hbm.at[:, LANES:], books.at[1], in_sem.at[3]),
    ]
    for copy in inputs:
        copy.start()

    barrier = pltpu.get_barrier_semaphore()

    def greet_plane(k, carry):
        target = ((dp + k // 2) % 16, 2 * plane + (core + k) % 2)
        pl.semaphore_signal(barrier, inc=1, device_id=target, device_id_type=MESH)
        return carry

    def greet_line(k, carry):
        target = (dp, 2 * ((plane + k // 2) % planes) + k % 2)
        pl.semaphore_signal(barrier, inc=1, device_id=target, device_id_type=MESH)
        return carry

    lax.fori_loop(1, 32, greet_plane, 0)
    lax.fori_loop(2, devices, greet_line, 0)

    def ids_part(where, which):
        return ids.at[where, :, pl.ds(pl.multiple_of(which * half, half), half)]

    def ids_copy(k):
        return remote(
            ids_part(8, core), ids_part((k + 1) // 2, core), ids_send.at[k], ids_recv.at[(k + 1) // 2, core],
            ((y + entry(MOVES, k, 0)) % 4 * 4 + (x + entry(MOVES, k, 1)) % 4, 2 * plane + keeper),
        )

    def ids_arrival(where, which):
        return remote(
            ids_part(8, which), ids_part(where, which), ids_send.at[0], ids_recv.at[where, which],
            (dp, 2 * plane + 1 - core),
        )

    def rs_copy(d, other):
        return remote(
            rs_out.at[d], rs_in.at[dp], rs_send.at[d, other], rs_recv.at[dp],
            (8 * core + d, 2 * plane + other),
        )

    def rs_away(d, other):
        return jnp.logical_or(8 * core + d != dp, other != core)

    def pair_copy(p):
        return remote(
            pair_out.at[p], pair_in.at[p], pair_send.at[p], pair_recv.at[p], (dp, 2 * plane + 1 - core)
        )

    def ag_copy(which, k):
        target = ((dp + k) % 16, dim)
        if which == 0:
            return remote(base.at[pl.ds(0, 3)], base_in.at[slot], ag_send.at[0, k], ag_recv.at[0, slot], target)
        return remote(base.at[3], last_in.at[slot], ag_send.at[1, k], ag_recv.at[1, slot], target)

    def ag_arrival(which, r):
        target = ((dp + 1) % 16, dim)
        if which == 0:
            return remote(base.at[pl.ds(0, 3)], base_in.at[r], ag_send.at[0, 0], ag_recv.at[0, r], target)
        return remote(base.at[3], last_in.at[r], ag_send.at[1, 0], ag_recv.at[1, r], target)

    def z_copy(k):
        return remote(z_out, z_in.at[dim], z_send.at[k], z_recv.at[dim], (dp, (dim + k) % devices))

    def z_arrival(k):
        return remote(z_out, z_in.at[k], z_send.at[0], z_recv.at[k], (dp, (dim + 1) % devices))

    def s_copy(k):
        return remote(s_out, s_in.at[dp], s_send.at[k], s_recv.at[dp], ((dp + k) % 16, dim))

    def s_arrival(k):
        return remote(s_out, s_in.at[k], s_send.at[0], s_recv.at[k], ((dp + 1) % 16, dim))

    def each(low_end, high_end, act):
        lax.fori_loop(low_end, high_end, lambda k, carry: (act(k), carry)[1], 0)

    def unless(skip, act):
        pl.when(jnp.logical_not(skip))(act)

    inputs[0].wait()
    pl.semaphore_wait(barrier, 31 + devices - 2)
    for k in range(7):
        ids_copy(k).start()

    make_masks(ids.at[8], low.at[8], high.at[8])
    for copy in inputs[1:]:
        copy.wait()
    forward_local(books, vec, ids.at[8], e_local)
    for d in range(8):
        e_rows[d] = e_local[d : d + 1, :]
        for h in range(2):
            rs_out[d, :, h * LANES : (h + 1) * LANES] = (RIDGE / 16) * books[h, pl.ds(d, 8, stride=8), :]


    def local_pass(k, carry):
        d = (slot + k) % 8
        found = extract(backward(low.at[8], high.at[8], e_rows.at[d]), fold)
        rs_out[d] = scale * found - rs_out[d]
        for other in range(2):
            pl.when(rs_away(d, other))(lambda: rs_copy(d, other).start())
        ids_copy(7 + k).start()
        return carry

    lax.fori_loop(0, 8, local_pass, 0)

    def place(q):
        return jnp.where(jnp.logical_and(kept, q == 0), 8, q)

    def arrival(q):
        where = place(q)

        @pl.when(where < 8)
        def _():
            ids_arrival(where, 0).wait_recv()
            ids_arrival(where, 1).wait_recv()
            make_masks(ids.at[where], low.at[where], high.at[where])

    each(0, EARLY, arrival)

    @pl.when(owned)
    def _():
        rs_in[dp] = rs_out[slot]

    each(0, 16, lambda k: unless(jnp.logical_and(owned, k == dp), lambda: remote(
        rs_out.at[0], rs_in.at[k], rs_send.at[0, 0], rs_recv.at[k], (dp, 2 * plane + 1 - core)).wait_recv()))
    terms = [rs_in[k] for k in range(16)]
    while len(terms) > 1:
        terms = [terms[k] + terms[k + 1] for k in range(0, len(terms), 2)]
    base[0] = terms[0]

    def join(p, found):
        pair_out[p] = scale * found
        pair_copy(p).start()

    def joined(p):
        pair_copy(p).wait_recv()
        base[p + 1] = (pair_out[p] + pair_in[p]) + (RIDGE - SHIFT) * base[p]

    def sweep():
        def two(q, total):
            first, second = place(2 * q), place(2 * q + 1)
            one = backward(low.at[first], high.at[first], e_rows.at[2 * q])
            other = backward(low.at[second], high.at[second], e_rows.at[2 * q + 1])
            return total + (one + other)

        return lax.fori_loop(0, 4, two, jnp.zeros((128, CODES), f32))

    def ahead(table, q, rows):
        for u in range(2):
            forward(table, ids.at[place(2 * q + u)], rows.at[u])

    def behind(q, rows):
        terms = []
        for u in range(2):
            where = place(2 * q + u)
            terms.append(backward(low.at[where], high.at[where], rows.at[u]))
        return terms[0] + terms[1]

    def fused(table):
        ahead(table, 0, e_even)

        def four(t, total):
            total = total + behind(2 * t, e_even)
            ahead(table, 2 * t + 1, e_odd)
            total = total + behind(2 * t + 1, e_odd)
            ahead(table, (2 * t + 2) % 4, e_even)
            return total

        return lax.fori_loop(0, 2, four, jnp.zeros((128, CODES), f32))

    def first(t, total):
        @pl.when(2 * t >= EARLY)
        def _():
            arrival(2 * t)
            arrival(2 * t + 1)

        ahead(base[0], t, e_even)
        return total + behind(t, e_even)

    join(0, extract(lax.fori_loop(0, 4, first, jnp.zeros((128, CODES), f32)), fold))
    joined(0)
    join(1, extract(fused(base[1]), fold))
    zero = jnp.zeros((8, LANES), f32)
    v0, v1 = base[0], base[1]
    sums = dots([(v0, v0), (v0, v1), (v1, v1)], 0, (zero, zero))
    joined(1)

    def last_forward(t, carry):
        blocks = []
        for q in (2 * t, 2 * t + 1):
            blocks += forward(base[2], ids.at[place(q)], e_rows.at[q], packed=True)
        return plus(carry, tree([two_prod(block, block) for block in blocks]))

    norm = lax.fori_loop(0, 4, last_forward, (zero, zero))
    v2 = base[2]
    sums = over_lanes(dots([(v0, v2), (v1, v2), (v2, v2)], 3, sums, [norm]))
    z_out[0:8] = sums[0]
    z_out[8:16] = sums[1]
    each(1, devices, lambda k: z_copy(k).start())
    z_in[dim] = z_out[...]

    @pl.when(owned)
    def _():
        each(1, 16, lambda k: ag_copy(0, k).start())
        base_in[slot] = base[0:3]

    join(2, extract(sweep(), fold))
    each(0, devices, lambda k: unless(k == dim, lambda: z_arrival(k).wait_recv()))
    sums = tree([(z_in[k, 0:8], z_in[k, 8:16]) for k in range(devices)])
    s_out[0:8] = sums[0]
    s_out[8:16] = sums[1]
    each(1, 16, lambda k: s_copy(k).start())
    s_in[dp] = s_out[...]
    joined(2)

    @pl.when(owned)
    def _():
        each(1, 16, lambda k: ag_copy(1, k).start())
        last_in[slot] = base[3]

    each(0, 16, lambda k: unless(k == dp, lambda: s_arrival(k).wait_recv()))
    c0, c1, c2 = solve(tree([(s_in[k, 0:8], s_in[k, 8:16]) for k in range(16)]), scale)
    one = (jnp.ones_like(c0[0]), jnp.zeros_like(c0[0]))
    q0 = minus(one, scaled(c0, SHIFT))[0]
    q1 = -plus(c0, scaled(c1, SHIFT))[0]
    q2 = -plus(c1, scaled(c2, SHIFT))[0]
    q3 = -c2[0]
    c0, c1, c2 = c0[0], c1[0], c2[0]

    def arrived(which, r):
        unless(jnp.logical_and(owned, r == slot), lambda: ag_arrival(which, r).wait_recv())

    each(0, 8, lambda r: arrived(0, r))
    for d in range(8):
        for h in range(2):
            lanes = slice(h * LANES, (h + 1) * LANES)
            rows = pl.ds(d, 8, stride=8)
            v0, v1, v2 = [base_in[d, k, :, lanes] for k in range(3)]
            x_out[h, rows, :] = books[h, rows, :] + (c0 * v0 + c1 * v1 + c2 * v2)
            base_in[d, 0, :, lanes] = q0 * v0 + q1 * v1 + q2 * v2
    def outgoing(which):
        source, target = ((x_out, x_hbm), (r_out, r_hbm))[which]
        return [
            pltpu.make_async_copy(
                source.at[h], target.at[:, h * LANES : (h + 1) * LANES], out_sem.at[2 * which + h]
            )
            for h in range(2)
        ]

    for copy in outgoing(0):
        copy.start()
    each(0, 8, lambda r: arrived(1, r))
    for d in range(8):
        for h in range(2):
            lanes = slice(h * LANES, (h + 1) * LANES)
            r_out[h, pl.ds(d, 8, stride=8), :] = base_in[d, 0, :, lanes] + q3 * last_in[d, :, lanes]

    for copy in outgoing(1):
        copy.start()

    each(0, 15, lambda k: ids_copy(k).wait_send())
    for other in range(2):
        each(0, 8, lambda d: pl.when(rs_away(d, other))(lambda: rs_copy(d, other).wait_send()))
    each(0, 3, lambda p: pair_copy(p).wait_send())
    each(1, devices, lambda k: z_copy(k).wait_send())
    each(1, 16, lambda k: s_copy(k).wait_send())

    @pl.when(owned)
    def _():
        each(1, 16, lambda k: ag_copy(0, k).wait_send())
        each(1, 16, lambda k: ag_copy(1, k).wait_send())

    for copy in outgoing(0) + outgoing(1):
        copy.wait()


def per_device(planes, vectors, code_ids, start_books):
    sections, width, codes = start_books.shape
    count = code_ids.shape[1]
    scale = codes / (count * 16)
    devices = 2 * planes
    rows = sections * width
    books = start_books.reshape(rows, codes)
    dma = pltpu.SemaphoreType.DMA
    flat = (rows, codes)
    halves = (2, rows, LANES)
    x, r = pl.pallas_call(
        functools.partial(kernel, planes, scale),
        out_shape=(jax.ShapeDtypeStruct(flat, f32),) * 2,
        in_specs=[pl.BlockSpec(memory_space=pl.ANY)] * 3,
        out_specs=(pl.BlockSpec(memory_space=pl.ANY),) * 2,
        scratch_shapes=[
            pltpu.VMEM((width, count), f32),
            pltpu.VMEM(halves, f32),
            pltpu.VMEM((9, sections, count), jnp.int32),
            pltpu.VMEM((9, 64, count), bf16),
            pltpu.VMEM((9, count, CODES), bf16),
            pltpu.VMEM((width, count), f32),
            pltpu.VMEM((8, 1, count), f32),
            pltpu.VMEM((2, 1, count), f32),
            pltpu.VMEM((2, 1, count), f32),
            pltpu.VMEM((64, LANES), f32),
            pltpu.VMEM((8, sections, CODES), f32),
            pltpu.VMEM((16, sections, CODES), f32),
            pltpu.VMEM((3, sections, CODES), f32),
            pltpu.VMEM((3, sections, CODES), f32),
            pltpu.VMEM((4, sections, CODES), f32),
            pltpu.VMEM((8, 3, sections, CODES), f32),
            pltpu.VMEM((8, sections, CODES), f32),
            pltpu.VMEM(halves, f32),
            pltpu.VMEM(halves, f32),
            pltpu.VMEM((16, LANES), f32),
            pltpu.VMEM((devices, 16, LANES), f32),
            pltpu.VMEM((16, LANES), f32),
            pltpu.VMEM((16, 16, LANES), f32),
            dma((4,)), dma((4,)), dma((16,)), dma((8, 2)), dma((8, 2)), dma((16,)), dma((3,)), dma((3,)),
            dma((2, 16)), dma((2, 8)), dma((devices,)), dma((devices,)), dma((16,)), dma((16,)),
        ],
        compiler_params=pltpu.CompilerParams(
            collective_id=0, has_side_effects=True, vmem_limit_bytes=61 << 20
        ),
    )(vectors, code_ids, books)

    return x.reshape(sections, width, codes), r.reshape(sections, width, codes)


def solution(mesh):
    return jax.shard_map(
        functools.partial(per_device, mesh.shape["dim"] // 2),
        mesh=mesh,
        in_specs=(P("dim", "dp"), P(None, "dp"), P(None, "dim", None)),
        out_specs=(P(None, "dim", None), P(None, "dim", None)),
        check_vma=False,
    )
```

```python
import functools

import jax
import jax.numpy as jnp
from jax import lax
from jax.experimental import pallas as pl
from jax.experimental.pallas import tpu as pltpu
from jax.sharding import PartitionSpec as P

f32 = jnp.float32
bf16 = jnp.bfloat16
MESH = pl.DeviceIdType.MESH
LANES = 128
SECTIONS = 8
CODES = 256
RIDGE = 0.5
SHIFT = 2.0
EVEN = ((0, 0), (1, 1), (3, 3), (1, 3), (3, 1), (0, 2), (2, 0), (2, 2))
ODD = ((0, 1), (0, 3), (1, 0), (3, 0), (2, 1), (2, 3), (1, 2), (3, 2))
MOVES = tuple(move for pair in zip(ODD, EVEN[1:]) for move in pair) + (ODD[7],)
EARLY = 6


def entry(table, k, which):
    if isinstance(k, int):
        return table[k][which]
    out = jnp.int32(table[0][which])
    for place in range(1, len(table)):
        out = jnp.where(k == place, table[place][which], out)
    return out


def two_sum(a, b):
    s = a + b
    t = s - a
    return s, (a - (s - t)) + (b - t)


def two_prod(a, b):
    p = a * b
    ca = a * 4097.0
    ah = ca - (ca - a)
    al = a - ah
    cb = b * 4097.0
    bh = cb - (cb - b)
    bl = b - bh
    return p, ((ah * bh - p) + ah * bl + al * bh) + al * bl


def tidy(h, r):
    s = h + r
    return s, r - (s - h)


def plus(a, b):
    s, e = two_sum(a[0], b[0])
    return tidy(s, e + (a[1] + b[1]))


def minus(a, b):
    return plus(a, (-b[0], -b[1]))


def times(a, b):
    p, e = two_prod(a[0], b[0])
    return tidy(p, e + (a[0] * b[1] + a[1] * b[0]))


def over(a, b):
    first = a[0] / b[0]
    rest = minus(a, times((first, jnp.zeros_like(first)), b))
    return tidy(first, rest[0] / b[0])


def scaled(a, power):
    return a[0] * power, a[1] * power


def pick(table, index):
    place = index & (LANES - 1)
    low = jnp.take_along_axis(table[0], place, axis=1)
    high = jnp.take_along_axis(table[1], place, axis=1)
    return jnp.where(index >= LANES, high, low)


def make_masks(ids_ref, low_ref, high_ref, chunk=2048):
    count = ids_ref.shape[1]
    row_low = lax.broadcasted_iota(jnp.int32, (64, chunk), 0) & 7
    row_high = lax.broadcasted_iota(jnp.int32, (CODES, chunk), 0) & 31

    def step(k, carry):
        span = pl.ds(pl.multiple_of(k * chunk, chunk), chunk)
        code = ids_ref[:, span]
        top = code >> 5
        wide = jnp.concatenate(
            [jnp.broadcast_to(top[m : m + 1], (8, chunk)) for m in range(SECTIONS)], axis=0
        )
        low_ref[:, span] = jnp.where(wide == row_low, 1.0, 0.0).astype(bf16)
        part = code & 31
        wide = jnp.concatenate(
            [jnp.broadcast_to(part[m : m + 1], (32, chunk)) for m in range(SECTIONS)], axis=0
        )
        high_ref[span, :] = jnp.where(wide == row_high, 1.0, 0.0).astype(bf16).T
        return carry

    lax.fori_loop(0, count // chunk, step, 0)


def forward_local(books_ref, vec_ref, ids_ref, e_ref):
    count = ids_ref.shape[1]

    def step(g, carry):
        span = pl.ds(pl.multiple_of(g * LANES, LANES), LANES)
        code = ids_ref[:, span]
        total = vec_ref[:, span]
        for m in range(SECTIONS):
            total = total - pick(
                (books_ref[0, 8 * m : 8 * m + 8, :], books_ref[1, 8 * m : 8 * m + 8, :]), jnp.broadcast_to(code[m : m + 1], (8, LANES))
            )
        e_ref[:, span] = total
        return carry

    lax.fori_loop(0, count // LANES, step, 0, unroll=8)


def forward(table, ids_ref, e_ref, packed=False):
    count = ids_ref.shape[1]
    row = lax.broadcasted_iota(jnp.int32, (8, LANES), 0)
    blocks = []
    table = (table[:, :LANES], table[:, LANES:])
    for g in range(count // LANES):
        span = slice(g * LANES, (g + 1) * LANES)
        e = jnp.sum(pick(table, ids_ref[:, span]), axis=0, keepdims=True)
        e_ref[:, span] = e
        if packed:
            wide = jnp.broadcast_to(e, (8, LANES))
            if g % 8 == 0:
                blocks.append(wide)
            else:
                blocks[-1] = jnp.where(row == g % 8, wide, blocks[-1])
    return blocks


def weighted(low, e_row):
    wide = jnp.broadcast_to(e_row, (16, e_row.shape[1]))
    first = wide.astype(bf16)
    second = (wide - first.astype(f32)).astype(bf16)
    return jnp.concatenate(
        [low * jnp.concatenate([first] * 4, axis=0), low * jnp.concatenate([second] * 4, axis=0)],
        axis=0,
    )


def backward(low_ref, high_ref, e_ref, size=2048):
    total = None
    for q in range(low_ref.shape[1] // size):
        span = slice(q * size, (q + 1) * size)
        rows = weighted(low_ref[:, span], e_ref[:, span])
        term = jnp.dot(rows, high_ref[span, :], preferred_element_type=f32)
        total = term if total is None else total + term
    return total


def extract(acc, fold_ref):
    both = acc[:64] + acc[64:]
    for m in range(SECTIONS):
        half = both[8 * m : 8 * m + 8, :LANES] if m < 4 else both[8 * m : 8 * m + 8, LANES:]
        fold_ref[8 * m : 8 * m + 8, :] = half if m % 4 == 0 else pltpu.roll(half, LANES - 32 * (m % 4), 1)
    block = lax.broadcasted_iota(jnp.int32, (8, LANES), 1) >> 5
    halves = []
    for h in range(2):
        out = None
        for q in range(4):
            piece = fold_ref[pl.ds(4 * h + q, 8, stride=8), :]
            out = piece if q == 0 else jnp.where(block == q, pltpu.roll(piece, 32 * q, 1), out)
        halves.append(out)
    return jnp.concatenate(halves, axis=1)


def dots(pairs, first, carry, extra=()):
    row = lax.broadcasted_iota(jnp.int32, (8, LANES), 0)
    found = []
    for a, b in pairs:
        left = two_prod(a[:, :LANES], b[:, :LANES])
        right = two_prod(a[:, LANES:], b[:, LANES:])
        found.append(scaled(plus(left, right), 0.5))
    high, rest = carry
    for q, pair in enumerate(found + list(extra)):
        for distance in (4, 2, 1):
            pair = plus(pair, (pltpu.roll(pair[0], distance, 0), pltpu.roll(pair[1], distance, 0)))
        high = jnp.where(row == first + q, pair[0], high)
        rest = jnp.where(row == first + q, pair[1], rest)
    return high, rest


def over_lanes(pair):
    for distance in (64, 32, 16, 8, 4, 2, 1):
        pair = plus(pair, (pltpu.roll(pair[0], distance, 1), pltpu.roll(pair[1], distance, 1)))
    return pair


def tree(terms):
    while len(terms) > 1:
        terms = [plus(terms[k], terms[k + 1]) for k in range(0, len(terms), 2)]
    return terms[0]


def solve(total, scale):
    d00, d01, d11, d02, d12, d22, norm = [(total[0][q : q + 1], total[1][q : q + 1]) for q in range(7)]
    w00 = plus(d01, scaled(d00, SHIFT))
    w01 = plus(d02, scaled(d01, SHIFT))
    w02 = plus(d12, scaled(d02, SHIFT))
    w11 = plus(d12, scaled(d11, SHIFT))
    w12 = plus(d22, scaled(d12, SHIFT))
    w22 = plus(scaled(norm, scale), scaled(d22, RIDGE))
    l1 = over(w01, w00)
    l2 = over(w02, w00)
    p1 = minus(w11, times(l1, w01))
    u12 = minus(w12, times(l2, w01))
    l3 = over(u12, p1)
    p2 = minus(minus(w22, times(l2, w02)), times(l3, u12))
    y1 = minus(d01, times(l1, d00))
    y2 = minus(minus(d02, times(l2, d00)), times(l3, y1))
    c2 = over(y2, p2)
    c1 = minus(over(y1, p1), times(l3, c2))
    c0 = minus(minus(over(d00, w00), times(l1, c1)), times(l2, c2))
    return c0, c1, c2


def kernel(
    planes, scale, vec_hbm, ids_hbm, books_hbm, x_hbm, r_hbm,
    vec, books, ids, low, high, e_local, e_rows, e_even, e_odd, fold,
    rs_out, rs_in, pair_out, pair_in, base, base_in, last_in, x_out, r_out,
    z_out, z_in, s_out, s_in,
    in_sem, out_sem, ids_send, ids_recv, rs_send, rs_recv, pair_send, pair_recv,
    ag_send, ag_recv, z_send, z_recv, s_send, s_recv,
):
    dp = lax.axis_index("dp")
    dim = lax.axis_index("dim")
    core = dim % 2
    plane = dim // 2
    y, x = dp // 4, dp % 4
    owner, slot = dp // 8, dp % 8
    owned = core == owner
    keeper = (y + x) % 2
    kept = core == keeper
    half = ids.shape[2] // 2
    devices = 2 * planes

    def remote(src, dst, send_sem, recv_sem, target):
        return pltpu.make_async_remote_copy(
            src_ref=src, dst_ref=dst, send_sem=send_sem, recv_sem=recv_sem,
            device_id=target, device_id_type=MESH,
        )

    inputs = [
        pltpu.make_async_copy(ids_hbm, ids.at[8], in_sem.at[0]),
        pltpu.make_async_copy(vec_hbm, vec, in_sem.at[1]),
        pltpu.make_async_copy(books_hbm.at[:, 0:LANES], books.at[0], in_sem.at[2]),
        pltpu.make_async_copy(books_hbm.at[:, LANES:], books.at[1], in_sem.at[3]),
    ]
    for copy in inputs:
        copy.start()

    barrier = pltpu.get_barrier_semaphore()

    for k in range(2, devices):
        target = (dp, 2 * lax.rem(plane + k // 2, planes) + k % 2)
        pl.semaphore_signal(barrier, inc=1, device_id=target, device_id_type=MESH)
    for k in range(1, 32):
        target = (lax.rem(dp + k // 2, 16), 2 * plane + lax.rem(core + k, 2))
        pl.semaphore_signal(barrier, inc=1, device_id=target, device_id_type=MESH)


    def ids_part(where, which):
        return ids.at[where, :, pl.ds(pl.multiple_of(which * half, half), half)]

    def ids_copy(k):
        return remote(
            ids_part(8, core), ids_part((k + 1) // 2, core), ids_send.at[k], ids_recv.at[(k + 1) // 2, core],
            ((y + entry(MOVES, k, 0)) % 4 * 4 + (x + entry(MOVES, k, 1)) % 4, 2 * plane + keeper),
        )

    def ids_arrival(where, which):
        return remote(
            ids_part(8, which), ids_part(where, which), ids_send.at[0], ids_recv.at[where, which],
            (dp, 2 * plane + 1 - core),
        )

    def rs_copy(d, other):
        return remote(
            rs_out.at[d], rs_in.at[dp], rs_send.at[d, other], rs_recv.at[dp],
            (8 * core + d, 2 * plane + other),
        )

    def rs_away(d, other):
        return jnp.logical_or(8 * core + d != dp, other != core)

    def pair_copy(p):
        return remote(
            pair_out.at[p], pair_in.at[p], pair_send.at[p], pair_recv.at[p], (dp, 2 * plane + 1 - core)
        )

    def ag_copy(which, k):
        target = (lax.rem(dp + k, 16), dim)
        if which == 0:
            return remote(base.at[pl.ds(0, 3)], base_in.at[slot], ag_send.at[0, k], ag_recv.at[0, slot], target)
        return remote(base.at[3], last_in.at[slot], ag_send.at[1, k], ag_recv.at[1, slot], target)

    def ag_arrival(which, r):
        target = ((dp + 1) % 16, dim)
        if which == 0:
            return remote(base.at[pl.ds(0, 3)], base_in.at[r], ag_send.at[0, 0], ag_recv.at[0, r], target)
        return remote(base.at[3], last_in.at[r], ag_send.at[1, 0], ag_recv.at[1, r], target)

    def z_copy(k):
        return remote(z_out, z_in.at[dim], z_send.at[k], z_recv.at[dim], (dp, lax.rem(dim + k, devices)))

    def z_arrival(k):
        return remote(z_out, z_in.at[k], z_send.at[0], z_recv.at[k], (dp, (dim + 1) % devices))

    def s_copy(k):
        return remote(s_out, s_in.at[dp], s_send.at[k], s_recv.at[dp], (lax.rem(dp + k, 16), dim))

    def s_arrival(k):
        return remote(s_out, s_in.at[k], s_send.at[0], s_recv.at[k], ((dp + 1) % 16, dim))

    def each(low_end, high_end, act):
        lax.fori_loop(low_end, high_end, lambda k, carry: (act(k), carry)[1], 0)

    def unless(skip, act):
        pl.when(jnp.logical_not(skip))(act)

    inputs[0].wait()
    pl.semaphore_wait(barrier, 31 + devices - 2)
    for k in range(7):
        ids_copy(k).start()

    make_masks(ids.at[8], low.at[8], high.at[8])
    for copy in inputs[1:]:
        copy.wait()
    forward_local(books, vec, ids.at[8], e_local)
    for d in range(8):
        e_rows[d] = e_local[d : d + 1, :]
        for h in range(2):
            rs_out[d, :, h * LANES : (h + 1) * LANES] = (RIDGE / 16) * books[h, pl.ds(d, 8, stride=8), :]


    def local_pass(k, carry):
        d = (slot + k) % 8
        found = extract(backward(low.at[8], high.at[8], e_rows.at[d]), fold)
        rs_out[d] = scale * found - rs_out[d]
        for other in range(2):
            pl.when(rs_away(d, other))(lambda: rs_copy(d, other).start())
        ids_copy(7 + k).start()
        return carry

    lax.fori_loop(0, 8, local_pass, 0)

    def place(q):
        return jnp.where(jnp.logical_and(kept, q == 0), 8, q)

    def arrival(q):
        where = place(q)

        @pl.when(where < 8)
        def _():
            ids_arrival(where, 0).wait_recv()
            ids_arrival(where, 1).wait_recv()
            make_masks(ids.at[where], low.at[where], high.at[where])

    each(0, EARLY, arrival)

    @pl.when(owned)
    def _():
        rs_in[dp] = rs_out[slot]

    each(0, 16, lambda k: unless(jnp.logical_and(owned, k == dp), lambda: remote(
        rs_out.at[0], rs_in.at[k], rs_send.at[0, 0], rs_recv.at[k], (dp, 2 * plane + 1 - core)).wait_recv()))
    terms = [rs_in[k] for k in range(16)]
    while len(terms) > 1:
        terms = [terms[k] + terms[k + 1] for k in range(0, len(terms), 2)]
    base[0] = terms[0]

    def join(p, found):
        pair_out[p] = scale * found
        pair_copy(p).start()

    def joined(p):
        pair_copy(p).wait_recv()
        base[p + 1] = (pair_out[p] + pair_in[p]) + (RIDGE - SHIFT) * base[p]

    def sweep():
        def two(q, total):
            first, second = place(2 * q), place(2 * q + 1)
            one = backward(low.at[first], high.at[first], e_rows.at[2 * q])
            other = backward(low.at[second], high.at[second], e_rows.at[2 * q + 1])
            return total + (one + other)

        return lax.fori_loop(0, 4, two, jnp.zeros((128, CODES), f32))

    def ahead(table, q, rows):
        for u in range(2):
            forward(table, ids.at[place(2 * q + u)], rows.at[u])

    def behind(q, rows):
        terms = []
        for u in range(2):
            where = place(2 * q + u)
            terms.append(backward(low.at[where], high.at[where], rows.at[u]))
        return terms[0] + terms[1]

    def fused(table):
        ahead(table, 0, e_even)

        def four(t, total):
            total = total + behind(2 * t, e_even)
            ahead(table, 2 * t + 1, e_odd)
            total = total + behind(2 * t + 1, e_odd)
            ahead(table, (2 * t + 2) % 4, e_even)
            return total

        return lax.fori_loop(0, 2, four, jnp.zeros((128, CODES), f32))

    def first(t, total):
        @pl.when(2 * t >= EARLY)
        def _():
            arrival(2 * t)
            arrival(2 * t + 1)

        ahead(base[0], t, e_even)
        return total + behind(t, e_even)

    join(0, extract(lax.fori_loop(0, 4, first, jnp.zeros((128, CODES), f32)), fold))
    joined(0)
    join(1, extract(fused(base[1]), fold))
    zero = jnp.zeros((8, LANES), f32)
    v0, v1 = base[0], base[1]
    sums = dots([(v0, v0), (v0, v1), (v1, v1)], 0, (zero, zero))
    joined(1)

    def last_forward(t, carry):
        blocks = []
        for q in (2 * t, 2 * t + 1):
            blocks += forward(base[2], ids.at[place(q)], e_rows.at[q], packed=True)
        return plus(carry, tree([two_prod(block, block) for block in blocks]))

    norm = lax.fori_loop(0, 4, last_forward, (zero, zero))
    v2 = base[2]
    sums = over_lanes(dots([(v0, v2), (v1, v2), (v2, v2)], 3, sums, [norm]))
    z_out[0:8] = sums[0]
    z_out[8:16] = sums[1]
    each(1, devices, lambda k: z_copy(k).start())
    z_in[dim] = z_out[...]

    @pl.when(owned)
    def _():
        each(1, 16, lambda k: ag_copy(0, k).start())
        base_in[slot] = base[0:3]

    join(2, extract(sweep(), fold))
    each(0, devices, lambda k: unless(k == dim, lambda: z_arrival(k).wait_recv()))
    sums = tree([(z_in[k, 0:8], z_in[k, 8:16]) for k in range(devices)])
    s_out[0:8] = sums[0]
    s_out[8:16] = sums[1]
    each(1, 16, lambda k: s_copy(k).start())
    s_in[dp] = s_out[...]
    joined(2)

    @pl.when(owned)
    def _():
        each(1, 16, lambda k: ag_copy(1, k).start())
        last_in[slot] = base[3]

    each(0, 16, lambda k: unless(k == dp, lambda: s_arrival(k).wait_recv()))
    c0, c1, c2 = solve(tree([(s_in[k, 0:8], s_in[k, 8:16]) for k in range(16)]), scale)
    one = (jnp.ones_like(c0[0]), jnp.zeros_like(c0[0]))
    q0 = minus(one, scaled(c0, SHIFT))[0]
    q1 = -plus(c0, scaled(c1, SHIFT))[0]
    q2 = -plus(c1, scaled(c2, SHIFT))[0]
    q3 = -c2[0]
    c0, c1, c2 = c0[0], c1[0], c2[0]

    def arrived(which, r):
        unless(jnp.logical_and(owned, r == slot), lambda: ag_arrival(which, r).wait_recv())

    each(0, 8, lambda r: arrived(0, r))
    for d in range(8):
        for h in range(2):
            lanes = slice(h * LANES, (h + 1) * LANES)
            rows = pl.ds(d, 8, stride=8)
            v0, v1, v2 = [base_in[d, k, :, lanes] for k in range(3)]
            x_out[h, rows, :] = books[h, rows, :] + (c0 * v0 + c1 * v1 + c2 * v2)
            base_in[d, 0, :, lanes] = q0 * v0 + q1 * v1 + q2 * v2
    def outgoing(which):
        source, target = ((x_out, x_hbm), (r_out, r_hbm))[which]
        return [
            pltpu.make_async_copy(
                source.at[h], target.at[:, h * LANES : (h + 1) * LANES], out_sem.at[2 * which + h]
            )
            for h in range(2)
        ]

    for copy in outgoing(0):
        copy.start()
    each(0, 8, lambda r: arrived(1, r))
    for d in range(8):
        for h in range(2):
            lanes = slice(h * LANES, (h + 1) * LANES)
            r_out[h, pl.ds(d, 8, stride=8), :] = base_in[d, 0, :, lanes] + q3 * last_in[d, :, lanes]

    for copy in outgoing(1):
        copy.start()

    each(0, 15, lambda k: ids_copy(k).wait_send())
    for other in range(2):
        each(0, 8, lambda d: pl.when(rs_away(d, other))(lambda: rs_copy(d, other).wait_send()))
    each(0, 3, lambda p: pair_copy(p).wait_send())
    each(1, devices, lambda k: z_copy(k).wait_send())
    each(1, 16, lambda k: s_copy(k).wait_send())

    @pl.when(owned)
    def _():
        each(1, 16, lambda k: ag_copy(0, k).wait_send())
        each(1, 16, lambda k: ag_copy(1, k).wait_send())

    for copy in outgoing(0) + outgoing(1):
        copy.wait()


def per_device(planes, vectors, code_ids, start_books):
    sections, width, codes = start_books.shape
    count = code_ids.shape[1]
    scale = codes / (count * 16)
    devices = 2 * planes
    rows = sections * width
    books = start_books.reshape(rows, codes)
    dma = pltpu.SemaphoreType.DMA
    flat = (rows, codes)
    halves = (2, rows, LANES)
    x, r = pl.pallas_call(
        functools.partial(kernel, planes, scale),
        out_shape=(jax.ShapeDtypeStruct(flat, f32),) * 2,
        in_specs=[pl.BlockSpec(memory_space=pl.ANY)] * 3,
        out_specs=(pl.BlockSpec(memory_space=pl.ANY),) * 2,
        scratch_shapes=[
            pltpu.VMEM((width, count), f32),
            pltpu.VMEM(halves, f32),
            pltpu.VMEM((9, sections, count), jnp.int32),
            pltpu.VMEM((9, 64, count), bf16),
            pltpu.VMEM((9, count, CODES), bf16),
            pltpu.VMEM((width, count), f32),
            pltpu.VMEM((8, 1, count), f32),
            pltpu.VMEM((2, 1, count), f32),
            pltpu.VMEM((2, 1, count), f32),
            pltpu.VMEM((64, LANES), f32),
            pltpu.VMEM((8, sections, CODES), f32),
            pltpu.VMEM((16, sections, CODES), f32),
            pltpu.VMEM((3, sections, CODES), f32),
            pltpu.VMEM((3, sections, CODES), f32),
            pltpu.VMEM((4, sections, CODES), f32),
            pltpu.VMEM((8, 3, sections, CODES), f32),
            pltpu.VMEM((8, sections, CODES), f32),
            pltpu.VMEM(halves, f32),
            pltpu.VMEM(halves, f32),
            pltpu.VMEM((16, LANES), f32),
            pltpu.VMEM((devices, 16, LANES), f32),
            pltpu.VMEM((16, LANES), f32),
            pltpu.VMEM((16, 16, LANES), f32),
            dma((4,)), dma((4,)), dma((16,)), dma((8, 2)), dma((8, 2)), dma((16,)), dma((3,)), dma((3,)),
            dma((2, 16)), dma((2, 8)), dma((devices,)), dma((devices,)), dma((16,)), dma((16,)),
        ],
        compiler_params=pltpu.CompilerParams(
            collective_id=0, has_side_effects=True, vmem_limit_bytes=61 << 20
        ),
    )(vectors, code_ids, books)

    return x.reshape(sections, width, codes), r.reshape(sections, width, codes)


def solution(mesh):
    return jax.shard_map(
        functools.partial(per_device, mesh.shape["dim"] // 2),
        mesh=mesh,
        in_specs=(P("dim", "dp"), P(None, "dp"), P(None, "dim", None)),
        out_specs=(P(None, "dim", None), P(None, "dim", None)),
        check_vma=False,
    )
```
